32 devices in a mesh: img: 8 (over y, x, core), slab: 4 (over z).
Axes of the slice: x: 2, y: 2, z: 4, core: 2. Of those that a mesh axis runs over, the one named last changes fastest.
Arguments:
- state: float32 [64, 2, 128, 4, 128], P('img', None, 'slab'), may hold values from -3 to 3
- sources: int32 [64, 2], replicated, may hold values from 0 to 63, as said below
- weight_index: int32 [64], P('img'), may hold values from 0 to 15
Outputs:
- moved: float32 [64, 2, 128, 4, 128], P('img', None, 'slab')
The draws below stay inside these ranges and needn't reach their ends.
Inputs may be any that keep to these rules, and one draw needn't show every extreme that they name: Among the 16 sources of the 8 new images of one device (aligned blocks), at most 2 lie among the 8 images of any one device, and in every draw exactly 2 do for some devices.
All inputs are finite; a program needn't handle non-finite values.
Results may differ from the reference program's by a relative error of at most 0.00022.
Values sent between devices are 32-bit elements; how exact they have to be, the bound alone decides.
A program may use at most 128 MiB of HBM per device.

```python
import jax
import jax.numpy as jnp
from jax import lax

IMG_DEV = 8
GX = 4
GY = 128
SLOTS = 2
WLEVELS = 16
IMAGES = 64
NZ = 128


def draw_sources(key, part):
    key = jax.random.fold_in(key, 11)
    blocks = IMAGES // IMG_DEV
    entries = 2 * IMG_DEV
    subkeys = jax.random.split(key, blocks)

    def one_block(subkey):
        first_key, second_key, third_key = jax.random.split(subkey, 3)
        senders = jax.random.permutation(first_key, blocks)
        positions = jnp.arange(entries, dtype=jnp.int32)
        picks = positions // SLOTS
        ordering = jax.random.permutation(second_key, entries)
        owners = senders[picks[ordering]]
        offsets = jax.random.randint(third_key, (entries,), 0, IMG_DEV)
        return (owners * IMG_DEV + offsets).astype(jnp.int32)
    return jax.vmap(one_block)(subkeys).reshape(IMAGES, 2)


def plant(drawn, key, least, largest):
    shape = drawn.shape
    index_at = [jax.random.randint(jax.random.fold_in(key, axis), (), 0, shape[axis]) for axis in range(len(shape))]
    drawn = drawn.at[tuple(index_at)].set(least)
    longest = shape.index(max(shape))
    index_at[longest] = (index_at[longest] + 1) % shape[longest]
    return drawn.at[tuple(index_at)].set(largest)


def block_scale(key, dims, cuts, least, high):
    factor_of = 1.0
    for dim, shards_of in cuts:
        draws = jax.random.uniform(jax.random.fold_in(jax.random.fold_in(key, 6), dim), (shards_of,), jnp.float32, least / len(cuts), high / len(cuts))
        factor_of = factor_of * jnp.repeat(jnp.exp(draws), dims[dim] // shards_of).reshape((-1,) + (1,) * (len(dims) - 1 - dim))
    return factor_of


def bell_draw(stream_key, dims, width, bound, cuts=(), kind=jnp.bfloat16):
    gain = block_scale(stream_key, dims, cuts, -0.22, 0.18) if cuts else 1.0
    values = jax.random.normal(stream_key, dims, jnp.float32) * width * gain
    return jnp.minimum(jnp.maximum(values, -bound), bound).astype(kind)


def setup_inputs(seed: int = 0) -> dict:
    keys = jax.random.split(jax.random.key(seed), 4)
    state = bell_draw(keys[0], (IMAGES, 2, NZ, GX, GY), 0.5, 3.0, ((0, 8), (2, 4)), jnp.float32)
    sources = draw_sources(jax.random.fold_in(keys[3], 71), 0)
    weight_index = plant(jax.random.randint(keys[2], (IMAGES,), 0, WLEVELS), jax.random.fold_in(keys[2], 1), 0, WLEVELS - 1).astype(jnp.int32)
    return dict(state=state, sources=sources, weight_index=weight_index)


KAPPA = 0.25
COUPLE = 0.3
STEP_SIZE = 0.004
EPSILON = 1e-06

def drift(phi, face):
    padded = jnp.pad(phi, ((0, 0), (1, 1), (0, 0), (0, 0)))
    lapl = padded[:, 2:] + padded[:, :-2]
    lapl = lapl + jnp.roll(phi, 1, 2) + jnp.roll(phi, -1, 2)
    lapl = lapl + jnp.roll(phi, 1, 3) + jnp.roll(phi, -1, 3) - 6.0 * phi
    potential = phi * phi * phi - phi + COUPLE * phi[::-1] - KAPPA * lapl
    mobile = 0.5 + 1.0 / (1.0 + phi * phi)
    total = jnp.zeros_like(phi)
    for axis_no in (2, 3):
        face_mob = 0.5 * (mobile + jnp.roll(mobile, -1, axis_no))
        flux = face_mob * (jnp.roll(potential, -1, axis_no) - potential)
        total = total + flux - jnp.roll(flux, 1, axis_no)
    face_z = 0.5 * (mobile[:, 1:] + mobile[:, :-1]) * face[None, :, None, None]
    flux_z = face_z * (potential[:, 1:] - potential[:, :-1])
    total = total + jnp.pad(flux_z, ((0, 0), (0, 1), (0, 0), (0, 0)))
    total = total - jnp.pad(flux_z, ((0, 0), (1, 0), (0, 0), (0, 0)))
    return total

def reference(state, sources, weight_index):
    images = state.shape[0]
    face = jnp.ones((state.shape[2] - 1,), jnp.float32)

    def update(index):
        before = lax.dynamic_index_in_dim(state, index - 1, 0, keepdims=False)
        current = lax.dynamic_index_in_dim(state, index, 0, keepdims=False)
        after = lax.dynamic_index_in_dim(state, index + 1, 0, keepdims=False)
        own_drift = drift(current, face)
        tangent = (after - before) * ((images - 1) / 2.0)
        second = (after - 2.0 * current + before) * float((images - 1) ** 2)
        scale = jnp.sqrt(jnp.sum(own_drift * own_drift)) / jnp.sqrt(jnp.sum(tangent * tangent) + EPSILON)
        moment = scale * tangent - own_drift
        _, back = jax.vjp(lambda field: drift(field, face), current)
        pulled = back(moment)[0]
        return current + STEP_SIZE * (scale * scale * second + pulled)
    inner = lax.map(update, jnp.arange(1, images - 1, dtype=jnp.int32))
    updated = jnp.concatenate([state[:1], inner, state[-1:]], axis=0)
    weights = (weight_index.astype(jnp.float32) + 1.0) / (WLEVELS + 1.0)

    def place(index):
        first = lax.dynamic_index_in_dim(updated, sources[index, 0], 0, keepdims=False)
        other = lax.dynamic_index_in_dim(updated, sources[index, 1], 0, keepdims=False)
        weight = weights[index]
        return weight * first + (1.0 - weight) * other
    return lax.map(place, jnp.arange(images, dtype=jnp.int32))
```

```python
import functools

import jax
import jax.numpy as jnp
from jax import lax
from jax.experimental import pallas as pl
from jax.experimental.pallas import tpu as pltpu
from jax.sharding import PartitionSpec as P

MESH = pl.DeviceIdType.MESH
WLEVELS = 16
KAPPA = 0.25
COUPLE = 0.3
STEP_SIZE = 0.004
EPSILON = 1e-06
SLOTS = 2
HALO = 4
RIM = 2


def kernel(
    n, m, per, depth, gx, chunks,
    state, sources, levels, out,
    land, edge, cells, mu_s, hm_s, b_s, t_s, sec_s, r_s, q_s, upd, sums, outbuf,
    pick, where_from, sbuf, *rest,
):
    rbufs = rest[:chunks]
    load_sem, out_sem, hs_sem, hr_sem, ss_sem, sr_sem, as_sem, ar_sem = rest[chunks:]
    me = lax.axis_index("img")
    slab = lax.axis_index("slab")
    entries = per * 2
    images = per * n
    planes = depth + 2 * HALO
    rows = gx * per
    own = depth * gx
    step = depth // chunks
    crow = step * gx

    def rem(a, b):
        return lax.rem(a, jnp.int32(b))

    nxt, prv = rem(me + 1, n), rem(me + n - 1, n)
    has_low, has_high = slab > 0, slab < m - 1

    def loads():
        return pltpu.make_async_copy(
            state, land.at[:, :, pl.ds(HALO * gx, own), :], load_sem
        )

    loads().start()

    barrier = pltpu.get_barrier_semaphore()

    def greet(i, s):
        pl.semaphore_signal(
            barrier, inc=1, device_id={"img": i, "slab": s}, device_id_type=MESH
        )

    for o in range(1, n):
        greet(rem(me + o, n), slab)
    for o in range(1, m):
        greet(me, rem(slab + o, m))

    @pl.when(has_low)
    def _():
        greet(nxt, slab - 1)
        greet(prv, slab - 1)

    @pl.when(has_high)
    def _():
        greet(nxt, slab + 1)
        greet(prv, slab + 1)

    count = (n - 1) + (m - 1) + jnp.where(has_low, 2, 0) + jnp.where(has_high, 2, 0)
    pl.semaphore_wait(barrier, count)

    def halo(k, src, dst, i, s):
        return pltpu.make_async_remote_copy(
            src_ref=src, dst_ref=dst, send_sem=hs_sem.at[k], recv_sem=hr_sem.at[k],
            device_id={"img": i, "slab": s}, device_id_type=MESH,
        )

    hr, rr, top = HALO * gx, RIM * gx, (HALO + depth) * gx
    last = per - 1
    to_high = [
        halo(0, state.at[:, :, pl.ds(own - hr, hr), :], land.at[:, :, pl.ds(0, hr), :], me, slab + 1),
        halo(4, state.at[last, :, pl.ds(own - rr, rr), :], edge.at[0, :, pl.ds(hr - rr, rr), :], nxt, slab + 1),
        halo(5, state.at[0, :, pl.ds(own - rr, rr), :], edge.at[1, :, pl.ds(hr - rr, rr), :], prv, slab + 1),
    ]
    to_low = [
        halo(1, state.at[:, :, pl.ds(0, hr), :], land.at[:, :, pl.ds(top, hr), :], me, slab - 1),
        halo(6, state.at[last, :, pl.ds(0, rr), :], edge.at[0, :, pl.ds(top, rr), :], nxt, slab - 1),
        halo(7, state.at[0, :, pl.ds(0, rr), :], edge.at[1, :, pl.ds(top, rr), :], prv, slab - 1),
    ]
    beside = [
        halo(2, state.at[last], edge.at[0, :, pl.ds(hr, own), :], nxt, slab),
        halo(3, state.at[0], edge.at[1, :, pl.ds(hr, own), :], prv, slab),
    ]

    @pl.when(has_high)
    def _():
        for c in to_high:
            c.start()

    @pl.when(has_low)
    def _():
        for c in to_low:
            c.start()

    for c in beside:
        c.start()

    def choose(d, carry):
        seen = jnp.int32(0)
        first = jnp.int32(0)
        second = jnp.int32(0)
        for e in range(entries):
            src = sources[d * per + e // 2, e % 2]
            mine = lax.div(src, jnp.int32(per)) == me
            place = lax.rem(src, jnp.int32(per))
            first = jnp.where(mine & (seen == 0), place, first)
            second = jnp.where(mine & (seen == 1), place, second)
            seen = seen + jnp.where(mine, 1, 0)
        pick[SLOTS * d] = first
        pick[SLOTS * d + 1] = second
        return carry

    lax.fori_loop(0, n, choose, 0)
    owners = []
    for e in range(entries):
        owner = lax.div(sources[me * per + e // 2, e % 2], jnp.int32(per))
        slot = jnp.int32(0)
        for before in owners:
            slot = jnp.where(before == owner, 1, slot)
        owners.append(owner)
        where_from[e] = SLOTS * owner + slot

    def rx(a, up):
        k = per if up else rows - per
        return jnp.concatenate([a[k:], a[:k]], axis=0)

    def ry(a, up):
        return pltpu.roll(a, a.shape[1] - 1 if up else 1, 1)

    def at(f, z):
        return pl.ds(pl.multiple_of((f * planes + z) * rows, 8), rows)

    def settle(lo, hi):
        def body(g, carry):
            for f in range(2):
                for i in range(per):
                    cells[pl.ds((f * planes + 2 * g) * rows + i, 8, stride=per), :] = land[
                        i, f, pl.ds(pl.multiple_of(8 * g, 8), 8), :
                    ]
            return carry

        lax.fori_loop(lo // 2, hi // 2, body, 0)

    def potentials(lo, hi):
        def body(z, carry):
            s = [cells[at(f, z), :] for f in range(2)]
            for f in range(2):
                a = s[f]
                sq = a * a
                near = cells[at(f, z + 1), :] + cells[at(f, z - 1), :]
                near = near + (rx(a, True) + rx(a, False)) + (ry(a, True) + ry(a, False))
                mu_s[at(f, z), :] = a * (sq + (6.0 * KAPPA - 1.0)) + COUPLE * s[1 - f] - KAPPA * near
                hm_s[at(f, z), :] = 0.25 + 0.5 / (1.0 + sq)
            return carry

        lax.fori_loop(lo, hi, body, 0)

    zero = jnp.zeros((rows, 128), jnp.float32)
    loads().wait()
    settle(HALO, HALO + depth)
    potentials(HALO + 1, HALO + depth - 1)

    @pl.when(has_low)
    def _():
        for k in range(3):
            halo(0, *((land.at[:, :, pl.ds(0, hr), :],) * 2), me, slab - 1).wait_recv() if k == 0 else \
                halo(3 + k, *((edge.at[k - 1, :, pl.ds(hr - rr, rr), :],) * 2), me, slab - 1).wait_recv()
        settle(0, HALO)

    @pl.when(has_high)
    def _():
        for k in range(3):
            halo(1, *((land.at[:, :, pl.ds(top, hr), :],) * 2), me, slab + 1).wait_recv() if k == 0 else \
                halo(5 + k, *((edge.at[k - 1, :, pl.ds(top, rr), :],) * 2), me, slab + 1).wait_recv()
        settle(HALO + depth, planes)

    @pl.when(jnp.logical_not(has_low))
    def _():
        for f in range(2):
            for z in range(HALO):
                cells[at(f, z), :] = zero
            for k in range(2):
                edge[k, f, pl.ds(hr - rr, rr), :] = zero[:rr]

    @pl.when(jnp.logical_not(has_high))
    def _():
        for f in range(2):
            for z in range(HALO + depth, planes):
                cells[at(f, z), :] = zero
            for k in range(2):
                edge[k, f, pl.ds(top, rr), :] = zero[:rr]

    potentials(1, HALO + 1)
    potentials(HALO + depth - 1, planes - 1)

    def mirror(ref):
        @pl.when(jnp.logical_not(has_low))
        def _():
            for f in range(2):
                ref[at(f, HALO - 1), :] = ref[at(f, HALO), :]

        @pl.when(jnp.logical_not(has_high))
        def _():
            for f in range(2):
                ref[at(f, HALO + depth), :] = ref[at(f, HALO + depth - 1), :]

    mirror(mu_s)
    for c in beside:
        c.wait_recv()

    line = lax.broadcasted_iota(jnp.int32, (per, 128), 0)
    at_last = line == per - 1
    at_first = line == 0

    def shifted(a, f, z):
        low, high = [], []
        for x in range(gx):
            tile = a[x * per : (x + 1) * per]
            r = pl.ds(z * gx + x, 1)
            before = jnp.broadcast_to(edge[0, f, r, :], (per, 128))
            after = jnp.broadcast_to(edge[1, f, r, :], (per, 128))
            low.append(pltpu.roll(jnp.where(at_last, before, tile), 1, 0))
            high.append(pltpu.roll(jnp.where(at_first, after, tile), per - 1, 0))
        return jnp.concatenate(low, axis=0), jnp.concatenate(high, axis=0)

    def fold(a):
        total = a[:per]
        for x in range(1, gx):
            total = total + a[x * per : (x + 1) * per]
        return total

    def z_flux(f, z):
        return (hm_s[at(f, z), :] + hm_s[at(f, z + 1), :]) * (mu_s[at(f, z + 1), :] - mu_s[at(f, z), :])

    def drifts(z, carry, summed):
        flux, acc_b, acc_t = list(carry[0:2]), carry[2], carry[3]
        for f in range(2):
            hm, mu = hm_s[at(f, z), :], mu_s[at(f, z), :]
            fz = (hm + hm_s[at(f, z + 1), :]) * (mu_s[at(f, z + 1), :] - mu)
            fx = (hm + rx(hm, True)) * (rx(mu, True) - mu)
            fy = (hm + ry(hm, True)) * (ry(mu, True) - mu)
            b = (fz - flux[f]) + (fx - rx(fx, False)) + (fy - ry(fy, False))
            flux[f] = fz
            a = cells[at(f, z), :]
            low, high = shifted(a, f, z)
            t = (high - low) * ((images - 1) / 2.0)
            b_s[at(f, z), :] = b
            t_s[at(f, z), :] = t
            sec_s[at(f, z), :] = (high + low - 2.0 * a) * float((images - 1) ** 2)
            if summed:
                acc_b = acc_b + fold(b * b)
                acc_t = acc_t + fold(t * t)
        return (flux[0], flux[1], acc_b, acc_t)

    none = jnp.zeros((per, 128), jnp.float32)
    carry = (z_flux(0, HALO - RIM - 1), z_flux(1, HALO - RIM - 1), none, none)
    carry = lax.fori_loop(HALO - RIM, HALO, lambda z, c: drifts(z, c, False), carry)
    carry = lax.fori_loop(HALO, HALO + depth, lambda z, c: drifts(z, c, True), carry)
    carry = lax.fori_loop(HALO + depth, HALO + depth + RIM, lambda z, c: drifts(z, c, False), carry)
    sums[0, 0] = carry[2]
    sums[0, 1] = carry[3]

    def share(o):
        return pltpu.make_async_remote_copy(
            src_ref=sums.at[0], dst_ref=sums.at[o], send_sem=ss_sem.at[o], recv_sem=sr_sem.at[o],
            device_id={"img": me, "slab": rem(slab + o, m)}, device_id_type=MESH,
        )

    for o in range(1, m):
        share(o).start()
    for o in range(1, m):
        share(o).wait_recv()
    total_b, total_t = sums[0, 0], sums[0, 1]
    for o in range(1, m):
        total_b = total_b + sums[o, 0]
        total_t = total_t + sums[o, 1]
    total_b = jnp.sum(total_b, axis=1, keepdims=True)
    total_t = jnp.sum(total_t, axis=1, keepdims=True)
    lam = jnp.sqrt(total_b) / jnp.sqrt(total_t + EPSILON)
    lam = jnp.broadcast_to(lam, (per, 128))
    ids = line + me * per
    inner = jnp.where((ids > 0) & (ids < images - 1), STEP_SIZE, 0.0).astype(jnp.float32)

    def wide(a):
        return jnp.concatenate([a] * gx, axis=0)

    lam_w, inner_w = wide(lam), wide(inner)
    square_w = wide(inner * lam * lam)

    def moments(z, carry):
        for f in range(2):
            t_s[at(f, z), :] = lam_w * t_s[at(f, z), :] - b_s[at(f, z), :]
        return carry

    lax.fori_loop(HALO - RIM, HALO + depth + RIM, moments, 0)
    mirror(t_s)

    def adjoint(z, carry):
        flux, prod = list(carry[0:2]), list(carry[2:4])
        for f in range(2):
            hm, mu, mo = hm_s[at(f, z), :], mu_s[at(f, z), :], t_s[at(f, z), :]
            dz = t_s[at(f, z + 1), :] - mo
            dx = rx(mo, True) - mo
            dy = ry(mo, True) - mo
            fz = (hm + hm_s[at(f, z + 1), :]) * dz
            fx = (hm + rx(hm, True)) * dx
            fy = (hm + ry(hm, True)) * dy
            pz = (mu_s[at(f, z + 1), :] - mu) * dz
            px = (rx(mu, True) - mu) * dx
            py = (ry(mu, True) - mu) * dy
            r_s[at(f, z), :] = (fz - flux[f]) + (fx - rx(fx, False)) + (fy - ry(fy, False))
            q_s[at(f, z), :] = (pz + prod[f]) + (px + rx(px, False)) + (py + ry(py, False))
            flux[f], prod[f] = fz, pz
        return (flux[0], flux[1], prod[0], prod[1])

    def finish(z, carry):
        r = [r_s[at(f, z), :] for f in range(2)]
        for f in range(2):
            a, c = cells[at(f, z), :], r[f]
            near = r_s[at(f, z + 1), :] + r_s[at(f, z - 1), :]
            near = near + (rx(c, True) + rx(c, False)) + (ry(c, True) + ry(c, False))
            inv = 2.0 * hm_s[at(f, z), :] - 0.5
            pulled = (3.0 * (a * a) + (6.0 * KAPPA - 1.0)) * c + COUPLE * r[1 - f] - KAPPA * near
            pulled = pulled + (a * inv) * (inv * q_s[at(f, z), :])
            upd[at(f, z), :] = a + (square_w * sec_s[at(f, z), :] + inner_w * pulled)
        return carry

    def pack(dest, c, put):
        for s in range(SLOTS):
            image = pick[SLOTS * dest + s]
            for f in range(2):
                for g in range(crow // 8):
                    start = (f * planes + HALO + c * step) * rows + g * 8 * per
                    put(s, f, pl.ds(8 * g, 8), upd[pl.ds(start + image, 8, stride=per), :])

    def send(c, o):
        return pltpu.make_async_remote_copy(
            src_ref=sbuf.at[c, o - 1], dst_ref=rbufs[c].at[pl.ds(SLOTS * me, SLOTS)],
            send_sem=as_sem.at[c, o], recv_sem=ar_sem.at[c, o],
            device_id={"img": rem(me + o, n), "slab": slab}, device_id_type=MESH,
        )

    def arrival(c, o):
        src = rem(me + n - o, n)
        return pltpu.make_async_remote_copy(
            src_ref=sbuf.at[c, o - 1], dst_ref=rbufs[c].at[pl.ds(SLOTS * src, SLOTS)],
            send_sem=as_sem.at[c, o], recv_sem=ar_sem.at[c, o],
            device_id={"img": src, "slab": slab}, device_id_type=MESH,
        )

    first = HALO - 2
    carry = []
    for f in range(2):
        dz = t_s[at(f, first + 1), :] - t_s[at(f, first), :]
        carry.append((hm_s[at(f, first), :] + hm_s[at(f, first + 1), :]) * dz)
    for f in range(2):
        dz = t_s[at(f, first + 1), :] - t_s[at(f, first), :]
        carry.append((mu_s[at(f, first + 1), :] - mu_s[at(f, first), :]) * dz)
    carry = tuple(carry)
    lo = HALO - 1
    for c in range(chunks):
        hi = HALO + (c + 1) * step + 1
        carry = lax.fori_loop(lo, hi, adjoint, carry)
        lo = hi
        if c == 0:
            @pl.when(jnp.logical_not(has_low))
            def _():
                for f in range(2):
                    r_s[at(f, HALO - 1), :] = zero
        if c == chunks - 1:
            @pl.when(jnp.logical_not(has_high))
            def _():
                for f in range(2):
                    r_s[at(f, HALO + depth), :] = zero
        lax.fori_loop(HALO + c * step, HALO + (c + 1) * step, finish, 0)
        for o in range(1, n):
            def put(s, f, where, value):
                sbuf[c, o - 1, s, f, where, :] = value

            pack(rem(me + o, n), c, put)
            send(c, o).start()

        def keep(s, f, where, value):
            rbufs[c][SLOTS * me + s, f, where, :] = value

        pack(me, c, keep)

    def store(c):
        return pltpu.make_async_copy(
            outbuf.at[:, :, pl.ds(c * crow, crow), :], out.at[:, :, pl.ds(c * crow, crow), :], out_sem.at[c]
        )

    for c in range(chunks):
        for o in range(1, n):
            arrival(c, o).wait_recv()
        for j in range(per):
            weight = (levels[j].astype(jnp.float32) + 1.0) * (1.0 / (WLEVELS + 1.0))
            one, two = where_from[2 * j], where_from[2 * j + 1]
            for f in range(2):
                outbuf[j, f, pl.ds(c * crow, crow), :] = (
                    weight * rbufs[c][one, f] + (1.0 - weight) * rbufs[c][two, f]
                )
        store(c).start()

    for c in range(chunks):
        for o in range(1, n):
            send(c, o).wait_send()
    for o in range(1, m):
        share(o).wait_send()
    for c in beside:
        c.wait_send()

    @pl.when(has_high)
    def _():
        for c in to_high:
            c.wait_send()

    @pl.when(has_low)
    def _():
        for c in to_low:
            c.wait_send()

    for c in range(chunks):
        store(c).wait()


def local(n, m, state, sources, levels):
    per, _, depth, gx, gy = state.shape
    planes = depth + 2 * HALO
    chunks = 4
    crow = depth // chunks * gx
    field = pltpu.VMEM((2 * planes * gx * per, gy), jnp.float32)
    flat = state.reshape(per, 2, depth * gx, gy)
    moved = pl.pallas_call(
        functools.partial(kernel, n, m, per, depth, gx, chunks),
        out_shape=jax.ShapeDtypeStruct(flat.shape, jnp.float32),
        in_specs=[
            pl.BlockSpec(memory_space=pl.ANY),
            pl.BlockSpec(memory_space=pltpu.SMEM),
            pl.BlockSpec(memory_space=pltpu.SMEM),
        ],
        out_specs=pl.BlockSpec(memory_space=pl.ANY),
        scratch_shapes=[
            pltpu.VMEM((per, 2, planes * gx, gy), jnp.float32),
            pltpu.VMEM((2, 2, planes * gx, gy), jnp.float32),
        ]
        + [field] * 9
        + [
            pltpu.VMEM((m, 2, per, gy), jnp.float32),
            pltpu.VMEM((per, 2, depth * gx, gy), jnp.float32),
            pltpu.SMEM((SLOTS * n,), jnp.int32),
            pltpu.SMEM((2 * per,), jnp.int32),
            pltpu.VMEM((chunks, n - 1, SLOTS, 2, crow, gy), jnp.float32),
        ]
        + [pltpu.VMEM((SLOTS * n, 2, crow, gy), jnp.float32)] * chunks
        + [
            pltpu.SemaphoreType.DMA,
            pltpu.SemaphoreType.DMA((chunks,)),
            pltpu.SemaphoreType.DMA((8,)),
            pltpu.SemaphoreType.DMA((8,)),
            pltpu.SemaphoreType.DMA((m,)),
            pltpu.SemaphoreType.DMA((m,)),
            pltpu.SemaphoreType.DMA((chunks, n)),
            pltpu.SemaphoreType.DMA((chunks, n)),
        ],
        compiler_params=pltpu.CompilerParams(
            collective_id=0, has_side_effects=True, vmem_limit_bytes=48 * 1024 * 1024
        ),
        cost_estimate=pl.CostEstimate(
            flops=110 * flat.size, bytes_accessed=8 * flat.size, transcendentals=flat.size
        ),
    )(flat, sources, levels)
    return moved.reshape(state.shape)


def solution(mesh):
    return jax.shard_map(
        functools.partial(local, mesh.shape["img"], mesh.shape["slab"]),
        mesh=mesh,
        in_specs=(P("img", None, "slab", None, None), P(), P("img")),
        out_specs=P("img", None, "slab", None, None),
        check_vma=False,
    )
```

```python
import functools

import jax
import jax.numpy as jnp
from jax import lax
from jax.experimental import pallas as pl
from jax.experimental.pallas import tpu as pltpu
from jax.sharding import PartitionSpec as P

MESH = pl.DeviceIdType.MESH
WLEVELS = 16
KAPPA = 0.25
COUPLE = 0.3
STEP_SIZE = 0.004
EPSILON = 1e-06
SLOTS = 2
HALO = 4
RIM = 2


def kernel(
    n, m, per, depth, gx, sizes,
    state, sources_hbm, levels_hbm, out,
    sources, levels, land, edge, cells, mu_s, hm_s, b_s, t_s, sec_s, r_s, q_s, upd, sums, outbuf,
    pick, where_from, sbuf, *rest,
):
    chunks = len(sizes)
    starts = [sum(sizes[:c]) for c in range(chunks)]
    sbufs, rbufs = (sbuf,) + rest[: chunks - 1], rest[chunks - 1 : 2 * chunks - 1]
    load_sem, out_sem, hs_sem, hr_sem, ss_sem, sr_sem, as_sem, ar_sem = rest[2 * chunks - 1 :]
    me = lax.axis_index("img")
    slab = lax.axis_index("slab")
    entries = per * 2
    images = per * n
    planes = depth + 2 * HALO
    rows = gx * per
    own = depth * gx

    def rem(a, b):
        return lax.rem(a, jnp.int32(b))

    nxt, prv = rem(me + 1, n), rem(me + n - 1, n)

    def partner(o):
        other, bit = me, 1
        while bit < n:
            if o & bit:
                other = other + bit - 2 * bit * rem(lax.div(me, jnp.int32(bit)), 2)
            bit *= 2
        return other

    order = sorted(range(1, n), key=lambda o: (o < 2, o % 2, -(o // 2)))
    has_low, has_high = slab > 0, slab < m - 1

    def loads():
        return pltpu.make_async_copy(
            state, land.at[:, :, pl.ds(HALO * gx, own), :], load_sem.at[0]
        )

    tables = [
        pltpu.make_async_copy(sources_hbm, sources, load_sem.at[1]),
        pltpu.make_async_copy(levels_hbm, levels, load_sem.at[2]),
    ]
    loads().start()
    for c in tables:
        c.start()

    barrier = pltpu.get_barrier_semaphore()

    def greet(i, s):
        pl.semaphore_signal(
            barrier, inc=1, device_id={"img": i, "slab": s}, device_id_type=MESH
        )

    for o in range(1, n):
        greet(partner(o), slab)
    for o in range(1, m):
        greet(me, rem(slab + o, m))

    @pl.when(has_low)
    def _():
        greet(nxt, slab - 1)
        greet(prv, slab - 1)

    @pl.when(has_high)
    def _():
        greet(nxt, slab + 1)
        greet(prv, slab + 1)

    count = (n - 1) + (m - 1) + jnp.where(has_low, 2, 0) + jnp.where(has_high, 2, 0)
    pl.semaphore_wait(barrier, count)

    def halo(k, src, dst, i, s):
        return pltpu.make_async_remote_copy(
            src_ref=src, dst_ref=dst, send_sem=hs_sem.at[k], recv_sem=hr_sem.at[k],
            device_id={"img": i, "slab": s}, device_id_type=MESH,
        )

    hr, rr, top = HALO * gx, RIM * gx, (HALO + depth) * gx
    last = per - 1
    to_high = [
        halo(0, state.at[:, :, pl.ds(own - hr, hr), :], land.at[:, :, pl.ds(0, hr), :], me, slab + 1),
        halo(4, state.at[last, :, pl.ds(own - rr, rr), :], edge.at[0, :, pl.ds(hr - rr, rr), :], nxt, slab + 1),
        halo(5, state.at[0, :, pl.ds(own - rr, rr), :], edge.at[1, :, pl.ds(hr - rr, rr), :], prv, slab + 1),
    ]
    to_low = [
        halo(1, state.at[:, :, pl.ds(0, hr), :], land.at[:, :, pl.ds(top, hr), :], me, slab - 1),
        halo(6, state.at[last, :, pl.ds(0, rr), :], edge.at[0, :, pl.ds(top, rr), :], nxt, slab - 1),
        halo(7, state.at[0, :, pl.ds(0, rr), :], edge.at[1, :, pl.ds(top, rr), :], prv, slab - 1),
    ]
    beside = [
        halo(2, state.at[last], edge.at[0, :, pl.ds(hr, own), :], nxt, slab),
        halo(3, state.at[0], edge.at[1, :, pl.ds(hr, own), :], prv, slab),
    ]

    @pl.when(has_high)
    def _():
        for c in to_high:
            c.start()

    @pl.when(has_low)
    def _():
        for c in to_low:
            c.start()

    for c in beside:
        c.start()

    def choose(d, carry):
        seen = jnp.int32(0)
        first = jnp.int32(0)
        second = jnp.int32(0)
        for e in range(entries):
            src = sources[e % 2, d * per + e // 2]
            mine = lax.div(src, jnp.int32(per)) == me
            place = lax.rem(src, jnp.int32(per))
            first = jnp.where(mine & (seen == 0), place, first)
            second = jnp.where(mine & (seen == 1), place, second)
            seen = seen + jnp.where(mine, 1, 0)
        pick[SLOTS * d] = first
        pick[SLOTS * d + 1] = second
        return carry

    for c in tables:
        c.wait()
    lax.fori_loop(0, n, choose, 0)
    owners = []
    for e in range(entries):
        owner = lax.div(sources[e % 2, me * per + e // 2], jnp.int32(per))
        slot = jnp.int32(0)
        for before in owners:
            slot = jnp.where(before == owner, 1, slot)
        owners.append(owner)
        where_from[e] = SLOTS * owner + slot

    def rx(a, up):
        k = per if up else rows - per
        return jnp.concatenate([a[k:], a[:k]], axis=0)

    def ry(a, up):
        return pltpu.roll(a, a.shape[1] - 1 if up else 1, 1)

    def at(f, z):
        start = (f * planes + z) * rows
        return pl.ds(start if isinstance(start, int) else pl.multiple_of(start, 8), rows)

    def loop(lo, hi, body, carry, k=2):
        full = (hi - lo) // k
        if full:
            carry = lax.fori_loop(0, full, lambda i, c: body(lo + i * k, c, k), carry)
        if lo + full * k < hi:
            carry = body(lo + full * k, carry, hi - lo - full * k)
        return carry

    def take(ref, z, j0, j1):
        return [{j: ref[at(f, z + j), :] for j in range(j0, j1)} for f in range(2)]

    def give(ref, z, values):
        for f in range(2):
            for j, v in values[f].items():
                ref[at(f, z + j), :] = v

    def settle(lo, hi):
        def body(g, carry):
            for f in range(2):
                for i in range(per):
                    cells[pl.ds((f * planes + 2 * g) * rows + i, 8, stride=per), :] = land[
                        i, f, pl.ds(pl.multiple_of(8 * g, 8), 8), :
                    ]
            return carry

        lax.fori_loop(lo // 2, hi // 2, body, 0)

    def potentials(lo, hi):
        def body(z, carry, k):
            s = take(cells, z, -1, k + 1)
            mu, hm = [{}, {}], [{}, {}]
            for j in range(k):
                for f in range(2):
                    a = s[f][j]
                    sq = a * a
                    near = (s[f][j + 1] + s[f][j - 1]) + (rx(a, True) + rx(a, False))
                    near = near + (ry(a, True) + ry(a, False))
                    mu[f][j] = a * (sq + (6.0 * KAPPA - 1.0)) + COUPLE * s[1 - f][j] - KAPPA * near
                    hm[f][j] = 0.25 + 0.5 / (1.0 + sq)
            give(mu_s, z, mu)
            give(hm_s, z, hm)
            return carry

        loop(lo, hi, body, 0)

    zero = jnp.zeros((rows, 128), jnp.float32)
    loads().wait()
    settle(HALO, HALO + depth)
    potentials(HALO + 1, HALO + depth - 1)

    @pl.when(has_low)
    def _():
        for k in range(3):
            halo(0, *((land.at[:, :, pl.ds(0, hr), :],) * 2), me, slab - 1).wait_recv() if k == 0 else \
                halo(3 + k, *((edge.at[k - 1, :, pl.ds(hr - rr, rr), :],) * 2), me, slab - 1).wait_recv()
        settle(0, HALO)

    @pl.when(has_high)
    def _():
        for k in range(3):
            halo(1, *((land.at[:, :, pl.ds(top, hr), :],) * 2), me, slab + 1).wait_recv() if k == 0 else \
                halo(5 + k, *((edge.at[k - 1, :, pl.ds(top, rr), :],) * 2), me, slab + 1).wait_recv()
        settle(HALO + depth, planes)

    @pl.when(jnp.logical_not(has_low))
    def _():
        for f in range(2):
            for z in range(HALO):
                cells[at(f, z), :] = zero
            for k in range(2):
                edge[k, f, pl.ds(hr - rr, rr), :] = zero[:rr]

    @pl.when(jnp.logical_not(has_high))
    def _():
        for f in range(2):
            for z in range(HALO + depth, planes):
                cells[at(f, z), :] = zero
            for k in range(2):
                edge[k, f, pl.ds(top, rr), :] = zero[:rr]

    potentials(1, HALO + 1)
    potentials(HALO + depth - 1, planes - 1)

    def mirror(ref):
        @pl.when(jnp.logical_not(has_low))
        def _():
            for f in range(2):
                ref[at(f, HALO - 1), :] = ref[at(f, HALO), :]

        @pl.when(jnp.logical_not(has_high))
        def _():
            for f in range(2):
                ref[at(f, HALO + depth), :] = ref[at(f, HALO + depth - 1), :]

    mirror(mu_s)
    for c in beside:
        c.wait_recv()

    line = lax.broadcasted_iota(jnp.int32, (per, 128), 0)
    at_last = line == per - 1
    at_first = line == 0

    def shifted(a, f, z):
        low, high = [], []
        for x in range(gx):
            tile = a[x * per : (x + 1) * per]
            r = pl.ds(z * gx + x, 1)
            before = jnp.broadcast_to(edge[0, f, r, :], (per, 128))
            after = jnp.broadcast_to(edge[1, f, r, :], (per, 128))
            low.append(pltpu.roll(jnp.where(at_last, before, tile), 1, 0))
            high.append(pltpu.roll(jnp.where(at_first, after, tile), per - 1, 0))
        return jnp.concatenate(low, axis=0), jnp.concatenate(high, axis=0)

    def fold(a):
        total = a[:per]
        for x in range(1, gx):
            total = total + a[x * per : (x + 1) * per]
        return total

    def z_flux(f, z):
        return (hm_s[at(f, z), :] + hm_s[at(f, z + 1), :]) * (mu_s[at(f, z + 1), :] - mu_s[at(f, z), :])

    def drifts(summed, z, carry, k):
        flux, acc_b, acc_t = list(carry[0:2]), carry[2], carry[3]
        hm, mu, s = take(hm_s, z, 0, k + 1), take(mu_s, z, 0, k + 1), take(cells, z, 0, k)
        near = [[shifted(s[f][j], f, z + j) for j in range(k)] for f in range(2)]
        b, t, sec = [{}, {}], [{}, {}], [{}, {}]
        for j in range(k):
            for f in range(2):
                h, u = hm[f][j], mu[f][j]
                fz = (h + hm[f][j + 1]) * (mu[f][j + 1] - u)
                fx = (h + rx(h, True)) * (rx(u, True) - u)
                fy = (h + ry(h, True)) * (ry(u, True) - u)
                b[f][j] = (fz - flux[f]) + (fx - rx(fx, False)) + (fy - ry(fy, False))
                flux[f] = fz
                low, high = near[f][j]
                t[f][j] = (high - low) * ((images - 1) / 2.0)
                sec[f][j] = (high + low - 2.0 * s[f][j]) * float((images - 1) ** 2)
                if summed:
                    acc_b = acc_b + fold(b[f][j] * b[f][j])
                    acc_t = acc_t + fold(t[f][j] * t[f][j])
        give(b_s, z, b)
        give(t_s, z, t)
        give(sec_s, z, sec)
        return (flux[0], flux[1], acc_b, acc_t)

    none = jnp.zeros((per, 128), jnp.float32)
    carry = (z_flux(0, HALO - RIM - 1), z_flux(1, HALO - RIM - 1), none, none)
    plain, summing = functools.partial(drifts, False), functools.partial(drifts, True)
    carry = loop(HALO - RIM, HALO, plain, carry)
    carry = loop(HALO, HALO + depth, summing, carry)
    carry = loop(HALO + depth, HALO + depth + RIM, plain, carry)
    sums[0, 0] = carry[2]
    sums[0, 1] = carry[3]

    def share(o):
        return pltpu.make_async_remote_copy(
            src_ref=sums.at[0], dst_ref=sums.at[o], send_sem=ss_sem.at[o], recv_sem=sr_sem.at[o],
            device_id={"img": me, "slab": rem(slab + o, m)}, device_id_type=MESH,
        )

    for o in range(1, m):
        share(o).start()
    mirror(t_s)
    mirror(b_s)
    for o in range(1, m):
        share(o).wait_recv()
    total_b, total_t = sums[0, 0], sums[0, 1]
    for o in range(1, m):
        total_b = total_b + sums[o, 0]
        total_t = total_t + sums[o, 1]
    total_b = jnp.sum(total_b, axis=1, keepdims=True)
    total_t = jnp.sum(total_t, axis=1, keepdims=True)
    lam = jnp.sqrt(total_b) / jnp.sqrt(total_t + EPSILON)
    lam = jnp.broadcast_to(lam, (per, 128))
    ids = line + me * per
    inner = jnp.where((ids > 0) & (ids < images - 1), STEP_SIZE, 0.0).astype(jnp.float32)

    def wide(a):
        return jnp.concatenate([a] * gx, axis=0)

    lam_w, inner_w = wide(lam), wide(inner)
    square_w = wide(inner * lam * lam)

    def moment(f, z):
        return lam_w * t_s[at(f, z), :] - b_s[at(f, z), :]

    def adjoint(z, carry, k):
        flux, prod = list(carry[0:2]), list(carry[2:4])
        hm, mu = take(hm_s, z, 0, k + 1), take(mu_s, z, 0, k + 1)
        mo = [{j: moment(f, z + j) for j in range(k + 1)} for f in range(2)]
        r, q = [{}, {}], [{}, {}]
        for j in range(k):
            for f in range(2):
                h, u, o = hm[f][j], mu[f][j], mo[f][j]
                dz, dx, dy = mo[f][j + 1] - o, rx(o, True) - o, ry(o, True) - o
                fz = (h + hm[f][j + 1]) * dz
                fx = (h + rx(h, True)) * dx
                fy = (h + ry(h, True)) * dy
                pz = (mu[f][j + 1] - u) * dz
                px = (rx(u, True) - u) * dx
                py = (ry(u, True) - u) * dy
                r[f][j] = (fz - flux[f]) + (fx - rx(fx, False)) + (fy - ry(fy, False))
                q[f][j] = (pz + prod[f]) + (px + rx(px, False)) + (py + ry(py, False))
                flux[f], prod[f] = fz, pz
        give(r_s, z, r)
        give(q_s, z, q)
        return (flux[0], flux[1], prod[0], prod[1])

    def finish(z, carry, k):
        r, s, hm = take(r_s, z, -1, k + 1), take(cells, z, 0, k), take(hm_s, z, 0, k)
        q, sec = take(q_s, z, 0, k), take(sec_s, z, 0, k)
        new = [{}, {}]
        for j in range(k):
            for f in range(2):
                a, c = s[f][j], r[f][j]
                near = (r[f][j + 1] + r[f][j - 1]) + (rx(c, True) + rx(c, False))
                near = near + (ry(c, True) + ry(c, False))
                inv = 2.0 * hm[f][j] - 0.5
                pulled = (3.0 * (a * a) + (6.0 * KAPPA - 1.0)) * c + COUPLE * r[1 - f][j] - KAPPA * near
                pulled = pulled + (a * inv) * (inv * q[f][j])
                new[f][j] = a + (square_w * sec[f][j] + inner_w * pulled)
        give(upd, z, new)
        return carry

    def pack(dest, c, put):
        for s in range(SLOTS):
            image = pick[SLOTS * dest + s]
            for f in range(2):
                for g in range(sizes[c] * gx // 8):
                    start = (f * planes + HALO + starts[c]) * rows + g * 8 * per
                    put(s, f, pl.ds(8 * g, 8), upd[pl.ds(start + image, 8, stride=per), :])

    def exchange(c, o, to):
        return pltpu.make_async_remote_copy(
            src_ref=sbufs[c].at[o - 1], dst_ref=rbufs[c].at[pl.ds(SLOTS * to, SLOTS)],
            send_sem=as_sem.at[c, o], recv_sem=ar_sem.at[c, o],
            device_id={"img": partner(o), "slab": slab}, device_id_type=MESH,
        )

    def send(c, o):
        return exchange(c, o, me)

    def arrival(c, o):
        return exchange(c, o, partner(o))

    first = HALO - 2
    dz = [moment(f, first + 1) - moment(f, first) for f in range(2)]
    carry = tuple(
        [(hm_s[at(f, first), :] + hm_s[at(f, first + 1), :]) * dz[f] for f in range(2)]
        + [(mu_s[at(f, first + 1), :] - mu_s[at(f, first), :]) * dz[f] for f in range(2)]
    )
    lo = HALO - 1
    for c in range(chunks):
        hi = HALO + starts[c] + sizes[c] + 1
        carry = loop(lo, hi, adjoint, carry)
        lo = hi
        if c == 0:
            @pl.when(jnp.logical_not(has_low))
            def _():
                for f in range(2):
                    r_s[at(f, HALO - 1), :] = zero
        if c == chunks - 1:
            @pl.when(jnp.logical_not(has_high))
            def _():
                for f in range(2):
                    r_s[at(f, HALO + depth), :] = zero
        loop(HALO + starts[c], HALO + starts[c] + sizes[c], finish, 0)
        for o in order:
            def put(s, f, where, value):
                sbufs[c][o - 1, s, f, where, :] = value

            pack(partner(o), c, put)
            send(c, o).start()

        def keep(s, f, where, value):
            rbufs[c][SLOTS * me + s, f, where, :] = value

        pack(me, c, keep)

    def store(c):
        part = pl.ds(starts[c] * gx, sizes[c] * gx)
        return pltpu.make_async_copy(outbuf.at[:, :, part, :], out.at[:, :, part, :], out_sem.at[c])

    for c in range(chunks):
        for o in order:
            arrival(c, o).wait_recv()
        for j in range(per):
            weight = (levels[j].astype(jnp.float32) + 1.0) * (1.0 / (WLEVELS + 1.0))
            one, two = where_from[2 * j], where_from[2 * j + 1]
            for f in range(2):
                outbuf[j, f, pl.ds(starts[c] * gx, sizes[c] * gx), :] = (
                    weight * rbufs[c][one, f] + (1.0 - weight) * rbufs[c][two, f]
                )
        store(c).start()

    for c in range(chunks):
        for o in range(1, n):
            send(c, o).wait_send()
    for o in range(1, m):
        share(o).wait_send()
    for c in beside:
        c.wait_send()

    @pl.when(has_high)
    def _():
        for c in to_high:
            c.wait_send()

    @pl.when(has_low)
    def _():
        for c in to_low:
            c.wait_send()

    for c in range(chunks):
        store(c).wait()


def local(n, m, state, sources, levels):
    per, _, depth, gx, gy = state.shape
    planes = depth + 2 * HALO
    sizes = (4, 8, 8, 8, 4)
    field = pltpu.VMEM((2 * planes * gx * per, gy), jnp.float32)
    flat = state.reshape(per, 2, depth * gx, gy)
    moved = pl.pallas_call(
        functools.partial(kernel, n, m, per, depth, gx, sizes),
        out_shape=jax.ShapeDtypeStruct(flat.shape, jnp.float32),
        in_specs=[pl.BlockSpec(memory_space=pltpu.HBM)] * 3,
        out_specs=pl.BlockSpec(memory_space=pl.ANY),
        scratch_shapes=[
            pltpu.SMEM((2, n * per), jnp.int32),
            pltpu.SMEM((per,), jnp.int32),
            pltpu.VMEM((per, 2, planes * gx, gy), jnp.float32),
            pltpu.VMEM((2, 2, planes * gx, gy), jnp.float32),
        ]
        + [field] * 9
        + [
            pltpu.VMEM((m, 2, per, gy), jnp.float32),
            pltpu.VMEM((per, 2, depth * gx, gy), jnp.float32),
            pltpu.SMEM((SLOTS * n,), jnp.int32),
            pltpu.SMEM((2 * per,), jnp.int32),
        ]
        + [pltpu.VMEM((n - 1, SLOTS, 2, k * gx, gy), jnp.float32) for k in sizes]
        + [pltpu.VMEM((SLOTS * n, 2, k * gx, gy), jnp.float32) for k in sizes]
        + [
            pltpu.SemaphoreType.DMA((3,)),
            pltpu.SemaphoreType.DMA((len(sizes),)),
            pltpu.SemaphoreType.DMA((8,)),
            pltpu.SemaphoreType.DMA((8,)),
            pltpu.SemaphoreType.DMA((m,)),
            pltpu.SemaphoreType.DMA((m,)),
            pltpu.SemaphoreType.DMA((len(sizes), n)),
            pltpu.SemaphoreType.DMA((len(sizes), n)),
        ],
        compiler_params=pltpu.CompilerParams(
            collective_id=0, has_side_effects=True, vmem_limit_bytes=63 * 1024 * 1024
        ),
        cost_estimate=pl.CostEstimate(
            flops=110 * flat.size, bytes_accessed=8 * flat.size, transcendentals=flat.size
        ),
    )(flat, sources.T, levels)
    return moved.reshape(state.shape)


def solution(mesh):
    return jax.shard_map(
        functools.partial(local, mesh.shape["img"], mesh.shape["slab"]),
        mesh=mesh,
        in_specs=(P("img", None, "slab", None, None), P(), P("img")),
        out_specs=P("img", None, "slab", None, None),
        check_vma=False,
    )
```

```python
import functools

import jax
import jax.numpy as jnp
from jax import lax
from jax.experimental import pallas as pl
from jax.experimental.pallas import tpu as pltpu
from jax.sharding import PartitionSpec as P

MESH = pl.DeviceIdType.MESH
WLEVELS = 16
KAPPA = 0.25
COUPLE = 0.3
STEP_SIZE = 0.004
EPSILON = 1e-06
SLOTS = 2
HALO = 4
RIM = 2


def kernel(
    n, m, per, depth, gx, chunks,
    state, sources_hbm, levels_hbm, out,
    sources, levels, land, edge, cells, mu_s, hm_s, b_s, t_s, sec_s, r_s, q_s, upd, sums, outbuf,
    pick, where_from, sbuf, *rest,
):
    rbufs = rest[:chunks]
    load_sem, out_sem, hs_sem, hr_sem, ss_sem, sr_sem, as_sem, ar_sem = rest[chunks:]
    me = lax.axis_index("img")
    slab = lax.axis_index("slab")
    entries = per * 2
    images = per * n
    planes = depth + 2 * HALO
    rows = gx * per
    step = depth // chunks
    crow = step * gx
    own = depth * gx

    def rem(a, b):
        return lax.rem(a, jnp.int32(b))

    nxt, prv = rem(me + 1, n), rem(me + n - 1, n)

    def partner(o):
        other, bit = me, 1
        while bit < n:
            flip = rem(lax.div(o, jnp.int32(bit)), 2)
            other = other + flip * (bit - 2 * bit * rem(lax.div(me, jnp.int32(bit)), 2))
            bit *= 2
        return other

    def each(body):
        def one(i, carry):
            body(n - 1 - i)
            return carry

        lax.fori_loop(0, n - 1, one, 0)

    has_low, has_high = slab > 0, slab < m - 1

    def loads():
        return pltpu.make_async_copy(
            state, land.at[:, :, pl.ds(HALO * gx, own), :], load_sem.at[0]
        )

    tables = [
        pltpu.make_async_copy(sources_hbm, sources, load_sem.at[1]),
        pltpu.make_async_copy(levels_hbm, levels, load_sem.at[2]),
    ]
    loads().start()
    for c in tables:
        c.start()

    barrier = pltpu.get_barrier_semaphore()

    def greet(i, s):
        pl.semaphore_signal(
            barrier, inc=1, device_id={"img": i, "slab": s}, device_id_type=MESH
        )

    each(lambda o: greet(partner(o), slab))
    for o in range(1, m):
        greet(me, rem(slab + o, m))

    @pl.when(has_low)
    def _():
        greet(nxt, slab - 1)
        greet(prv, slab - 1)

    @pl.when(has_high)
    def _():
        greet(nxt, slab + 1)
        greet(prv, slab + 1)

    count = (n - 1) + (m - 1) + jnp.where(has_low, 2, 0) + jnp.where(has_high, 2, 0)
    pl.semaphore_wait(barrier, count)
    for c in tables:
        c.wait()

    def halo(k, src, dst, i, s):
        return pltpu.make_async_remote_copy(
            src_ref=src, dst_ref=dst, send_sem=hs_sem.at[k], recv_sem=hr_sem.at[k],
            device_id={"img": i, "slab": s}, device_id_type=MESH,
        )

    hr, rr, top = HALO * gx, RIM * gx, (HALO + depth) * gx
    last = per - 1
    to_high = [
        halo(0, state.at[:, :, pl.ds(own - hr, hr), :], land.at[:, :, pl.ds(0, hr), :], me, slab + 1),
        halo(4, state.at[last, :, pl.ds(own - rr, rr), :], edge.at[0, :, pl.ds(hr - rr, rr), :], nxt, slab + 1),
        halo(5, state.at[0, :, pl.ds(own - rr, rr), :], edge.at[1, :, pl.ds(hr - rr, rr), :], prv, slab + 1),
    ]
    to_low = [
        halo(1, state.at[:, :, pl.ds(0, hr), :], land.at[:, :, pl.ds(top, hr), :], me, slab - 1),
        halo(6, state.at[last, :, pl.ds(0, rr), :], edge.at[0, :, pl.ds(top, rr), :], nxt, slab - 1),
        halo(7, state.at[0, :, pl.ds(0, rr), :], edge.at[1, :, pl.ds(top, rr), :], prv, slab - 1),
    ]
    beside = [
        halo(2, state.at[last], edge.at[0, :, pl.ds(hr, own), :], nxt, slab),
        halo(3, state.at[0], edge.at[1, :, pl.ds(hr, own), :], prv, slab),
    ]

    @pl.when(has_high)
    def _():
        for c in to_high:
            c.start()

    @pl.when(has_low)
    def _():
        for c in to_low:
            c.start()

    for c in beside:
        c.start()

    def rx(a, up):
        k = per if up else rows - per
        return jnp.concatenate([a[k:], a[:k]], axis=0)

    def ry(a, up):
        return pltpu.roll(a, a.shape[1] - 1 if up else 1, 1)

    def at(f, z):
        start = (f * planes + z) * rows
        return pl.ds(start if isinstance(start, int) else pl.multiple_of(start, 8), rows)

    def loop(lo, hi, body, carry, k=2):
        full = (hi - lo) // k
        if full:
            carry = lax.fori_loop(0, full, lambda i, c: body(lo + i * k, c, k), carry)
        if lo + full * k < hi:
            carry = body(lo + full * k, carry, hi - lo - full * k)
        return carry

    def take(ref, z, j0, j1):
        return [{j: ref[at(f, z + j), :] for j in range(j0, j1)} for f in range(2)]

    def give(ref, z, values):
        for f in range(2):
            for j, v in values[f].items():
                ref[at(f, z + j), :] = v

    def settle(lo, hi):
        def body(g, carry):
            for f in range(2):
                for i in range(per):
                    cells[pl.ds((f * planes + 2 * g) * rows + i, 8, stride=per), :] = land[
                        i, f, pl.ds(pl.multiple_of(8 * g, 8), 8), :
                    ]
            return carry

        lax.fori_loop(lo // 2, hi // 2, body, 0)

    def potentials():
        def body(z, carry, k):
            s = take(cells, z, -1, k + 1)
            mu, hm = [{}, {}], [{}, {}]
            for j in range(k):
                for f in range(2):
                    a = s[f][j]
                    sq = a * a
                    near = (s[f][j + 1] + s[f][j - 1]) + (rx(a, True) + rx(a, False))
                    near = near + (ry(a, True) + ry(a, False))
                    mu[f][j] = a * (sq + (6.0 * KAPPA - 1.0)) + COUPLE * s[1 - f][j] - KAPPA * near
                    hm[f][j] = 0.25 + 0.5 / (1.0 + sq)
            give(mu_s, z, mu)
            give(hm_s, z, hm)
            return carry

        return body

    zero = jnp.zeros((rows, 128), jnp.float32)
    loads().wait()
    settle(HALO, HALO + depth)
    potential = potentials()
    loop(HALO + 1, HALO + depth - 1, potential, 0, 3)

    @pl.when(has_low)
    def _():
        for k in range(3):
            halo(0, *((land.at[:, :, pl.ds(0, hr), :],) * 2), me, slab - 1).wait_recv() if k == 0 else \
                halo(3 + k, *((edge.at[k - 1, :, pl.ds(hr - rr, rr), :],) * 2), me, slab - 1).wait_recv()
        settle(0, HALO)

    @pl.when(has_high)
    def _():
        for k in range(3):
            halo(1, *((land.at[:, :, pl.ds(top, hr), :],) * 2), me, slab + 1).wait_recv() if k == 0 else \
                halo(5 + k, *((edge.at[k - 1, :, pl.ds(top, rr), :],) * 2), me, slab + 1).wait_recv()
        settle(HALO + depth, planes)

    @pl.when(jnp.logical_not(has_low))
    def _():
        for f in range(2):
            for z in range(HALO):
                cells[at(f, z), :] = zero
            for k in range(2):
                edge[k, f, pl.ds(hr - rr, rr), :] = zero[:rr]

    @pl.when(jnp.logical_not(has_high))
    def _():
        for f in range(2):
            for z in range(HALO + depth, planes):
                cells[at(f, z), :] = zero
            for k in range(2):
                edge[k, f, pl.ds(top, rr), :] = zero[:rr]

    lax.fori_loop(0, 2, lambda i, c: potential(1 + i * (HALO + depth - 2), c, HALO), 0)

    def mirror(ref):
        @pl.when(jnp.logical_not(has_low))
        def _():
            for f in range(2):
                ref[at(f, HALO - 1), :] = ref[at(f, HALO), :]

        @pl.when(jnp.logical_not(has_high))
        def _():
            for f in range(2):
                ref[at(f, HALO + depth), :] = ref[at(f, HALO + depth - 1), :]

    mirror(mu_s)
    for c in beside:
        c.wait_recv()

    line = lax.broadcasted_iota(jnp.int32, (per, 128), 0)
    at_last = line == per - 1
    at_first = line == 0

    def shifted(a, f, z):
        low, high = [], []
        for x in range(gx):
            tile = a[x * per : (x + 1) * per]
            r = pl.ds(z * gx + x, 1)
            before = jnp.broadcast_to(edge[0, f, r, :], (per, 128))
            after = jnp.broadcast_to(edge[1, f, r, :], (per, 128))
            low.append(pltpu.roll(jnp.where(at_last, before, tile), 1, 0))
            high.append(pltpu.roll(jnp.where(at_first, after, tile), per - 1, 0))
        return jnp.concatenate(low, axis=0), jnp.concatenate(high, axis=0)

    def fold(a):
        total = a[:per]
        for x in range(1, gx):
            total = total + a[x * per : (x + 1) * per]
        return total

    def z_flux(f, z):
        return (hm_s[at(f, z), :] + hm_s[at(f, z + 1), :]) * (mu_s[at(f, z + 1), :] - mu_s[at(f, z), :])

    def drifts(z, carry, k):
        flux, acc_b, acc_t = list(carry[0:2]), carry[2], carry[3]
        hm, mu, s = take(hm_s, z, 0, k + 1), take(mu_s, z, 0, k + 1), take(cells, z, 0, k)
        near = [[shifted(s[f][j], f, z + j) for j in range(k)] for f in range(2)]
        b, t, sec = [{}, {}], [{}, {}], [{}, {}]
        for j in range(k):
            for f in range(2):
                h, u = hm[f][j], mu[f][j]
                fz = (h + hm[f][j + 1]) * (mu[f][j + 1] - u)
                fx = (h + rx(h, True)) * (rx(u, True) - u)
                fy = (h + ry(h, True)) * (ry(u, True) - u)
                b[f][j] = (fz - flux[f]) + (fx - rx(fx, False)) + (fy - ry(fy, False))
                flux[f] = fz
                low, high = near[f][j]
                t[f][j] = (high - low) * ((images - 1) / 2.0)
                sec[f][j] = (high + low - 2.0 * s[f][j]) * float((images - 1) ** 2)
                inside = (z + j >= HALO) & (z + j < HALO + depth)
                counts = jnp.where(inside, jnp.float32(1.0), jnp.float32(0.0))
                acc_b = acc_b + counts * fold(b[f][j] * b[f][j])
                acc_t = acc_t + counts * fold(t[f][j] * t[f][j])
        give(b_s, z, b)
        give(t_s, z, t)
        give(sec_s, z, sec)
        return (flux[0], flux[1], acc_b, acc_t)

    none = jnp.zeros((per, 128), jnp.float32)
    carry = (z_flux(0, HALO - RIM - 1), z_flux(1, HALO - RIM - 1), none, none)
    carry = loop(HALO - RIM, HALO + depth + RIM, drifts, carry, 4)
    sums[0, 0] = carry[2]
    sums[0, 1] = carry[3]

    def share(o):
        return pltpu.make_async_remote_copy(
            src_ref=sums.at[0], dst_ref=sums.at[o], send_sem=ss_sem.at[o], recv_sem=sr_sem.at[o],
            device_id={"img": me, "slab": rem(slab + o, m)}, device_id_type=MESH,
        )

    for o in range(1, m):
        share(o).start()
    mirror(t_s)
    mirror(b_s)

    def choose(d, carry):
        seen = jnp.int32(0)
        first = jnp.int32(0)
        second = jnp.int32(0)
        for e in range(entries):
            src = sources[e % 2, d * per + e // 2]
            mine = lax.div(src, jnp.int32(per)) == me
            place = lax.rem(src, jnp.int32(per))
            first = jnp.where(mine & (seen == 0), place, first)
            second = jnp.where(mine & (seen == 1), place, second)
            seen = seen + jnp.where(mine, 1, 0)
        pick[SLOTS * d] = first
        pick[SLOTS * d + 1] = second
        return carry

    lax.fori_loop(0, n, choose, 0)
    owners = []
    for e in range(entries):
        owner = lax.div(sources[e % 2, me * per + e // 2], jnp.int32(per))
        slot = jnp.int32(0)
        for before in owners:
            slot = jnp.where(before == owner, 1, slot)
        owners.append(owner)
        where_from[e] = SLOTS * owner + slot

    for o in range(1, m):
        share(o).wait_recv()
    total_b, total_t = sums[0, 0], sums[0, 1]
    for o in range(1, m):
        total_b = total_b + sums[o, 0]
        total_t = total_t + sums[o, 1]
    total_b = jnp.sum(total_b, axis=1, keepdims=True)
    total_t = jnp.sum(total_t, axis=1, keepdims=True)
    lam = jnp.sqrt(total_b) / jnp.sqrt(total_t + EPSILON)
    lam = jnp.broadcast_to(lam, (per, 128))
    ids = line + me * per
    inner = jnp.where((ids > 0) & (ids < images - 1), STEP_SIZE, 0.0).astype(jnp.float32)

    def wide(a):
        return jnp.concatenate([a] * gx, axis=0)

    lam_w, inner_w = wide(lam), wide(inner)
    square_w = wide(inner * lam * lam)

    def moment(f, z):
        return lam_w * t_s[at(f, z), :] - b_s[at(f, z), :]

    def adjoint(z, carry, k):
        flux, prod = list(carry[0:2]), list(carry[2:4])
        hm, mu = take(hm_s, z, 0, k + 1), take(mu_s, z, 0, k + 1)
        mo = [{j: moment(f, z + j) for j in range(k + 1)} for f in range(2)]
        r, q = [{}, {}], [{}, {}]
        for j in range(k):
            for f in range(2):
                h, u, o = hm[f][j], mu[f][j], mo[f][j]
                dz, dx, dy = mo[f][j + 1] - o, rx(o, True) - o, ry(o, True) - o
                fz = (h + hm[f][j + 1]) * dz
                fx = (h + rx(h, True)) * dx
                fy = (h + ry(h, True)) * dy
                pz = (mu[f][j + 1] - u) * dz
                px = (rx(u, True) - u) * dx
                py = (ry(u, True) - u) * dy
                r[f][j] = (fz - flux[f]) + (fx - rx(fx, False)) + (fy - ry(fy, False))
                q[f][j] = (pz + prod[f]) + (px + rx(px, False)) + (py + ry(py, False))
                flux[f], prod[f] = fz, pz
        give(r_s, z, r)
        give(q_s, z, q)
        return (flux[0], flux[1], prod[0], prod[1])

    def finish(z, carry, k):
        r, s, hm = take(r_s, z, -1, k + 1), take(cells, z, 0, k), take(hm_s, z, 0, k)
        q, sec = take(q_s, z, 0, k), take(sec_s, z, 0, k)
        new = [{}, {}]
        for j in range(k):
            for f in range(2):
                a, c = s[f][j], r[f][j]
                near = (r[f][j + 1] + r[f][j - 1]) + (rx(c, True) + rx(c, False))
                near = near + (ry(c, True) + ry(c, False))
                inv = 2.0 * hm[f][j] - 0.5
                pulled = (3.0 * (a * a) + (6.0 * KAPPA - 1.0)) * c + COUPLE * r[1 - f][j] - KAPPA * near
                pulled = pulled + (a * inv) * (inv * q[f][j])
                new[f][j] = a + (square_w * sec[f][j] + inner_w * pulled)
        give(upd, z, new)
        return carry

    def pack(dest, c, put):
        for s in range(SLOTS):
            image = pick[SLOTS * dest + s]
            for f in range(2):
                for g in range(crow // 8):
                    start = (f * planes + HALO + c * step) * rows + g * 8 * per
                    put(s, f, pl.ds(8 * g, 8), upd[pl.ds(start + image, 8, stride=per), :])

    def exchange(c, o, to):
        return pltpu.make_async_remote_copy(
            src_ref=sbuf.at[c, o - 1], dst_ref=rbufs[c].at[pl.ds(SLOTS * to, SLOTS)],
            send_sem=as_sem.at[c, o], recv_sem=ar_sem.at[c, o],
            device_id={"img": partner(o), "slab": slab}, device_id_type=MESH,
        )

    first = HALO - 2
    dz = [moment(f, first + 1) - moment(f, first) for f in range(2)]
    carry = tuple(
        [(hm_s[at(f, first), :] + hm_s[at(f, first + 1), :]) * dz[f] for f in range(2)]
        + [(mu_s[at(f, first + 1), :] - mu_s[at(f, first), :]) * dz[f] for f in range(2)]
    )
    carry = adjoint(HALO - 1, carry, 2)

    @pl.when(jnp.logical_not(has_low))
    def _():
        for f in range(2):
            r_s[at(f, HALO - 1), :] = zero

    def chunk(c, carry):
        z = HALO + c * step
        carry = lax.fori_loop(0, step // 2, lambda i, a: adjoint(z + 1 + 2 * i, a, 2), carry)

        @pl.when(jnp.logical_not(has_high) & (c == chunks - 1))
        def _():
            for f in range(2):
                r_s[at(f, HALO + depth), :] = zero

        lax.fori_loop(0, step // 2, lambda i, a: finish(z + 2 * i, a, 2), 0)

        def fill(o):
            def put(s, f, where, value):
                sbuf[c, o - 1, s, f, where, :] = value

            pack(partner(o), c, put)

        each(fill)
        for k in range(chunks):
            @pl.when(c == k)
            def _():
                each(lambda o: exchange(k, o, me).start())

                def keep(s, f, where, value):
                    rbufs[k][SLOTS * me + s, f, where, :] = value

                pack(me, k, keep)

        return carry

    lax.fori_loop(0, chunks, chunk, carry)

    def store(c):
        part = pl.ds(c * crow, crow)
        return pltpu.make_async_copy(outbuf.at[:, :, part, :], out.at[:, :, part, :], out_sem.at[c])

    for c in range(chunks):
        each(lambda o: exchange(c, o, partner(o)).wait_recv())

        def blend(j, carry):
            weight = (levels[j].astype(jnp.float32) + 1.0) * (1.0 / (WLEVELS + 1.0))
            one, two = where_from[2 * j], where_from[2 * j + 1]
            for f in range(2):
                outbuf[j, f, pl.ds(c * crow, crow), :] = (
                    weight * rbufs[c][one, f] + (1.0 - weight) * rbufs[c][two, f]
                )
            return carry

        lax.fori_loop(0, per, blend, 0)
        store(c).start()

    for c in range(chunks):
        each(lambda o: exchange(c, o, me).wait_send())
        store(c).wait()
    for o in range(1, m):
        share(o).wait_send()
    for c in beside:
        c.wait_send()

    @pl.when(has_high)
    def _():
        for c in to_high:
            c.wait_send()

    @pl.when(has_low)
    def _():
        for c in to_low:
            c.wait_send()


def local(n, m, state, sources, levels):
    per, _, depth, gx, gy = state.shape
    planes = depth + 2 * HALO
    chunks = depth // 4
    crow = depth // chunks * gx
    field = pltpu.VMEM((2 * planes * gx * per, gy), jnp.float32)
    flat = state.reshape(per, 2, depth * gx, gy)
    moved = pl.pallas_call(
        functools.partial(kernel, n, m, per, depth, gx, chunks),
        out_shape=jax.ShapeDtypeStruct(flat.shape, jnp.float32),
        in_specs=[pl.BlockSpec(memory_space=pltpu.HBM)] * 3,
        out_specs=pl.BlockSpec(memory_space=pl.ANY),
        scratch_shapes=[
            pltpu.SMEM((2, n * per), jnp.int32),
            pltpu.SMEM((per,), jnp.int32),
            pltpu.VMEM((per, 2, planes * gx, gy), jnp.float32),
            pltpu.VMEM((2, 2, planes * gx, gy), jnp.float32),
        ]
        + [field] * 9
        + [
            pltpu.VMEM((m, 2, per, gy), jnp.float32),
            pltpu.VMEM((per, 2, depth * gx, gy), jnp.float32),
            pltpu.SMEM((SLOTS * n,), jnp.int32),
            pltpu.SMEM((2 * per,), jnp.int32),
        ]
        + [pltpu.VMEM((chunks, n - 1, SLOTS, 2, crow, gy), jnp.float32)]
        + [pltpu.VMEM((SLOTS * n, 2, crow, gy), jnp.float32)] * chunks
        + [
            pltpu.SemaphoreType.DMA((3,)),
            pltpu.SemaphoreType.DMA((chunks,)),
            pltpu.SemaphoreType.DMA((8,)),
            pltpu.SemaphoreType.DMA((8,)),
            pltpu.SemaphoreType.DMA((m,)),
            pltpu.SemaphoreType.DMA((m,)),
            pltpu.SemaphoreType.DMA((chunks, n)),
            pltpu.SemaphoreType.DMA((chunks, n)),
        ],
        compiler_params=pltpu.CompilerParams(
            collective_id=0, has_side_effects=True, vmem_limit_bytes=48 * 1024 * 1024
        ),
        cost_estimate=pl.CostEstimate(
            flops=110 * flat.size, bytes_accessed=8 * flat.size, transcendentals=flat.size
        ),
    )(*(pltpu.with_memory_space_constraint(x, pltpu.HBM) for x in (flat, sources.T, levels)))
    return moved.reshape(state.shape)


def solution(mesh):
    return jax.shard_map(
        functools.partial(local, mesh.shape["img"], mesh.shape["slab"]),
        mesh=mesh,
        in_specs=(P("img", None, "slab", None, None), P(), P("img")),
        out_specs=P("img", None, "slab", None, None),
        check_vma=False,
    )
```

```python
import functools

import jax
import jax.numpy as jnp
from jax import lax
from jax.experimental import pallas as pl
from jax.experimental.pallas import tpu as pltpu
from jax.sharding import PartitionSpec as P

MESH = pl.DeviceIdType.MESH
WLEVELS = 16
KAPPA = 0.25
COUPLE = 0.3
STEP_SIZE = 0.004
EPSILON = 1e-06
SLOTS = 2
HALO = 4
RIM = 2


def kernel(
    n, m, per, depth, gx, chunks,
    state, sources_hbm, levels_hbm, out,
    sources, levels, land, edge, cells, mu_s, hm_s, b_s, t_s, sec_s, r_s, q_s, upd, sums, outbuf,
    pick, where_from, sbuf, *rest,
):
    rbufs = rest[:chunks]
    load_sem, out_sem, hs_sem, hr_sem, ss_sem, sr_sem, as_sem, ar_sem = rest[chunks:]
    me = lax.axis_index("img")
    slab = lax.axis_index("slab")
    entries = per * 2
    images = per * n
    planes = depth + 2 * HALO
    rows = gx * per
    step = depth // chunks
    crow = step * gx
    own = depth * gx

    def rem(a, b):
        return lax.rem(a, jnp.int32(b))

    nxt, prv = rem(me + 1, n), rem(me + n - 1, n)

    bits = [1 << k for k in range(n.bit_length() - 1)]
    turns = [bit - 2 * bit * rem(lax.div(me, jnp.int32(bit)), 2) for bit in bits]

    def partner(o):
        other = me
        for bit, turn in zip(bits, turns):
            other = other + rem(lax.div(o, jnp.int32(bit)), 2) * turn
        return other

    def each(body):
        def one(i, carry):
            body(n - 1 - i)
            return carry

        lax.fori_loop(0, n - 1, one, 0)

    has_low, has_high = slab > 0, slab < m - 1

    def loads():
        return pltpu.make_async_copy(
            state, land.at[:, :, pl.ds(HALO * gx, own), :], load_sem.at[0]
        )

    tables = [
        pltpu.make_async_copy(sources_hbm, sources, load_sem.at[1]),
        pltpu.make_async_copy(levels_hbm, levels, load_sem.at[2]),
    ]
    loads().start()
    for c in tables:
        c.start()

    barrier = pltpu.get_barrier_semaphore()

    def greet(i, s):
        pl.semaphore_signal(
            barrier, inc=1, device_id={"img": i, "slab": s}, device_id_type=MESH
        )

    each(lambda o: greet(partner(o), slab))
    for o in range(1, m):
        greet(me, rem(slab + o, m))

    @pl.when(has_low)
    def _():
        greet(nxt, slab - 1)
        greet(prv, slab - 1)

    @pl.when(has_high)
    def _():
        greet(nxt, slab + 1)
        greet(prv, slab + 1)

    count = (n - 1) + (m - 1) + jnp.where(has_low, 2, 0) + jnp.where(has_high, 2, 0)
    def settle(lo, hi):
        def body(g, carry):
            for f in range(2):
                for i in range(per):
                    cells[pl.ds((f * planes + 2 * g) * rows + i, 8, stride=per), :] = land[
                        i, f, pl.ds(pl.multiple_of(8 * g, 8), 8), :
                    ]
            return carry

        lax.fori_loop(lo // 2, hi // 2, body, 0)

    loads().wait()
    settle(HALO, HALO + depth)
    pl.semaphore_wait(barrier, count)
    for c in tables:
        c.wait()

    def halo(k, src, dst, i, s):
        return pltpu.make_async_remote_copy(
            src_ref=src, dst_ref=dst, send_sem=hs_sem.at[k], recv_sem=hr_sem.at[k],
            device_id={"img": i, "slab": s}, device_id_type=MESH,
        )

    hr, rr, top = HALO * gx, RIM * gx, (HALO + depth) * gx
    last = per - 1
    to_high = [
        halo(0, state.at[:, :, pl.ds(own - hr, hr), :], land.at[:, :, pl.ds(0, hr), :], me, slab + 1),
        halo(4, state.at[last, :, pl.ds(own - rr, rr), :], edge.at[0, :, pl.ds(hr - rr, rr), :], nxt, slab + 1),
        halo(5, state.at[0, :, pl.ds(own - rr, rr), :], edge.at[1, :, pl.ds(hr - rr, rr), :], prv, slab + 1),
    ]
    to_low = [
        halo(1, state.at[:, :, pl.ds(0, hr), :], land.at[:, :, pl.ds(top, hr), :], me, slab - 1),
        halo(6, state.at[last, :, pl.ds(0, rr), :], edge.at[0, :, pl.ds(top, rr), :], nxt, slab - 1),
        halo(7, state.at[0, :, pl.ds(0, rr), :], edge.at[1, :, pl.ds(top, rr), :], prv, slab - 1),
    ]
    beside = [
        halo(2, state.at[last], edge.at[0, :, pl.ds(hr, own), :], nxt, slab),
        halo(3, state.at[0], edge.at[1, :, pl.ds(hr, own), :], prv, slab),
    ]

    @pl.when(has_high)
    def _():
        for c in to_high:
            c.start()

    @pl.when(has_low)
    def _():
        for c in to_low:
            c.start()

    for c in beside:
        c.start()

    def rx(a, up):
        k = per if up else rows - per
        return jnp.concatenate([a[k:], a[:k]], axis=0)

    def ry(a, up):
        return pltpu.roll(a, a.shape[1] - 1 if up else 1, 1)

    def at(f, z):
        start = (f * planes + z) * rows
        return pl.ds(start if isinstance(start, int) else pl.multiple_of(start, 8), rows)

    def loop(lo, hi, body, carry, k=2):
        full = (hi - lo) // k
        if full:
            carry = lax.fori_loop(0, full, lambda i, c: body(lo + i * k, c, k), carry)
        if lo + full * k < hi:
            carry = body(lo + full * k, carry, hi - lo - full * k)
        return carry

    def take(ref, z, j0, j1):
        return [{j: ref[at(f, z + j), :] for j in range(j0, j1)} for f in range(2)]

    def give(ref, z, values):
        for f in range(2):
            for j, v in values[f].items():
                ref[at(f, z + j), :] = v

    def potentials():
        def body(z, carry, k):
            s = take(cells, z, -1, k + 1)
            mu, hm = [{}, {}], [{}, {}]
            for j in range(k):
                for f in range(2):
                    a = s[f][j]
                    sq = a * a
                    near = (s[f][j + 1] + s[f][j - 1]) + (rx(a, True) + rx(a, False))
                    near = near + (ry(a, True) + ry(a, False))
                    mu[f][j] = a * (sq + (6.0 * KAPPA - 1.0)) + COUPLE * s[1 - f][j] - KAPPA * near
                    hm[f][j] = 0.25 + 0.5 / (1.0 + sq)
            give(mu_s, z, mu)
            give(hm_s, z, hm)
            return carry

        return body

    zero = jnp.zeros((rows, 128), jnp.float32)
    potential = potentials()
    loop(HALO + 1, HALO + depth - 1, potential, 0, 3)

    @pl.when(has_low)
    def _():
        for k in range(3):
            halo(0, *((land.at[:, :, pl.ds(0, hr), :],) * 2), me, slab - 1).wait_recv() if k == 0 else \
                halo(3 + k, *((edge.at[k - 1, :, pl.ds(hr - rr, rr), :],) * 2), me, slab - 1).wait_recv()
        settle(0, HALO)

    @pl.when(has_high)
    def _():
        for k in range(3):
            halo(1, *((land.at[:, :, pl.ds(top, hr), :],) * 2), me, slab + 1).wait_recv() if k == 0 else \
                halo(5 + k, *((edge.at[k - 1, :, pl.ds(top, rr), :],) * 2), me, slab + 1).wait_recv()
        settle(HALO + depth, planes)

    @pl.when(jnp.logical_not(has_low))
    def _():
        for f in range(2):
            for z in range(HALO):
                cells[at(f, z), :] = zero
            for k in range(2):
                edge[k, f, pl.ds(hr - rr, rr), :] = zero[:rr]

    @pl.when(jnp.logical_not(has_high))
    def _():
        for f in range(2):
            for z in range(HALO + depth, planes):
                cells[at(f, z), :] = zero
            for k in range(2):
                edge[k, f, pl.ds(top, rr), :] = zero[:rr]

    lax.fori_loop(0, 2, lambda i, c: potential(1 + i * (HALO + depth - 2), c, HALO), 0)

    def mirror(ref):
        @pl.when(jnp.logical_not(has_low))
        def _():
            for f in range(2):
                ref[at(f, HALO - 1), :] = ref[at(f, HALO), :]

        @pl.when(jnp.logical_not(has_high))
        def _():
            for f in range(2):
                ref[at(f, HALO + depth), :] = ref[at(f, HALO + depth - 1), :]

    mirror(mu_s)
    for c in beside:
        c.wait_recv()

    line = lax.broadcasted_iota(jnp.int32, (per, 128), 0)
    at_last = line == per - 1
    at_first = line == 0

    def shifted(a, f, z):
        low, high = [], []
        for x in range(gx):
            tile = a[x * per : (x + 1) * per]
            r = pl.ds(z * gx + x, 1)
            before = jnp.broadcast_to(edge[0, f, r, :], (per, 128))
            after = jnp.broadcast_to(edge[1, f, r, :], (per, 128))
            low.append(pltpu.roll(jnp.where(at_last, before, tile), 1, 0))
            high.append(pltpu.roll(jnp.where(at_first, after, tile), per - 1, 0))
        return jnp.concatenate(low, axis=0), jnp.concatenate(high, axis=0)

    def fold(a):
        total = a[:per]
        for x in range(1, gx):
            total = total + a[x * per : (x + 1) * per]
        return total

    def z_flux(f, z):
        return (hm_s[at(f, z), :] + hm_s[at(f, z + 1), :]) * (mu_s[at(f, z + 1), :] - mu_s[at(f, z), :])

    def drifts(z, carry, k):
        flux, acc_b, acc_t = list(carry[0:2]), carry[2], carry[3]
        hm, mu, s = take(hm_s, z, 0, k + 1), take(mu_s, z, 0, k + 1), take(cells, z, 0, k)
        near = [[shifted(s[f][j], f, z + j) for j in range(k)] for f in range(2)]
        b, t, sec = [{}, {}], [{}, {}], [{}, {}]
        for j in range(k):
            for f in range(2):
                h, u = hm[f][j], mu[f][j]
                fz = (h + hm[f][j + 1]) * (mu[f][j + 1] - u)
                fx = (h + rx(h, True)) * (rx(u, True) - u)
                fy = (h + ry(h, True)) * (ry(u, True) - u)
                b[f][j] = (fz - flux[f]) + (fx - rx(fx, False)) + (fy - ry(fy, False))
                flux[f] = fz
                low, high = near[f][j]
                t[f][j] = (high - low) * ((images - 1) / 2.0)
                sec[f][j] = (high + low - 2.0 * s[f][j]) * float((images - 1) ** 2)
                inside = (z + j >= HALO) & (z + j < HALO + depth)
                counts = jnp.where(inside, jnp.float32(1.0), jnp.float32(0.0))
                acc_b = acc_b + counts * fold(b[f][j] * b[f][j])
                acc_t = acc_t + counts * fold(t[f][j] * t[f][j])
        give(b_s, z, b)
        give(t_s, z, t)
        give(sec_s, z, sec)
        return (flux[0], flux[1], acc_b, acc_t)

    none = jnp.zeros((per, 128), jnp.float32)
    carry = (z_flux(0, HALO - RIM - 1), z_flux(1, HALO - RIM - 1), none, none)
    carry = loop(HALO - RIM, HALO + depth + RIM, drifts, carry, 4)
    sums[0, 0] = carry[2]
    sums[0, 1] = carry[3]

    def share(o):
        return pltpu.make_async_remote_copy(
            src_ref=sums.at[0], dst_ref=sums.at[o], send_sem=ss_sem.at[o], recv_sem=sr_sem.at[o],
            device_id={"img": me, "slab": rem(slab + o, m)}, device_id_type=MESH,
        )

    for o in range(1, m):
        share(o).start()
    mirror(t_s)
    mirror(b_s)

    def choose(d, carry):
        seen = jnp.int32(0)
        first = jnp.int32(0)
        second = jnp.int32(0)
        for e in range(entries):
            src = sources[e % 2, d * per + e // 2]
            mine = lax.div(src, jnp.int32(per)) == me
            place = lax.rem(src, jnp.int32(per))
            first = jnp.where(mine & (seen == 0), place, first)
            second = jnp.where(mine & (seen == 1), place, second)
            seen = seen + jnp.where(mine, 1, 0)
        pick[SLOTS * d] = first
        pick[SLOTS * d + 1] = second
        return carry

    lax.fori_loop(0, n, choose, 0)
    owners = []
    for e in range(entries):
        owner = lax.div(sources[e % 2, me * per + e // 2], jnp.int32(per))
        slot = jnp.int32(0)
        for before in owners:
            slot = jnp.where(before == owner, 1, slot)
        owners.append(owner)
        where_from[e] = SLOTS * owner + slot

    for o in range(1, m):
        share(o).wait_recv()
    total_b, total_t = sums[0, 0], sums[0, 1]
    for o in range(1, m):
        total_b = total_b + sums[o, 0]
        total_t = total_t + sums[o, 1]
    total_b = jnp.sum(total_b, axis=1, keepdims=True)
    total_t = jnp.sum(total_t, axis=1, keepdims=True)
    lam = jnp.sqrt(total_b) / jnp.sqrt(total_t + EPSILON)
    lam = jnp.broadcast_to(lam, (per, 128))
    ids = line + me * per
    inner = jnp.where((ids > 0) & (ids < images - 1), STEP_SIZE, 0.0).astype(jnp.float32)

    def wide(a):
        return jnp.concatenate([a] * gx, axis=0)

    lam_w, inner_w = wide(lam), wide(inner)
    square_w = wide(inner * lam * lam)

    def moment(f, z):
        return lam_w * t_s[at(f, z), :] - b_s[at(f, z), :]

    def adjoint(z, carry, k):
        flux, prod = list(carry[0:2]), list(carry[2:4])
        hm, mu = take(hm_s, z, 0, k + 1), take(mu_s, z, 0, k + 1)
        mo = [{j: moment(f, z + j) for j in range(k + 1)} for f in range(2)]
        r, q = [{}, {}], [{}, {}]
        for j in range(k):
            for f in range(2):
                h, u, o = hm[f][j], mu[f][j], mo[f][j]
                dz, dx, dy = mo[f][j + 1] - o, rx(o, True) - o, ry(o, True) - o
                fz = (h + hm[f][j + 1]) * dz
                fx = (h + rx(h, True)) * dx
                fy = (h + ry(h, True)) * dy
                pz = (mu[f][j + 1] - u) * dz
                px = (rx(u, True) - u) * dx
                py = (ry(u, True) - u) * dy
                r[f][j] = (fz - flux[f]) + (fx - rx(fx, False)) + (fy - ry(fy, False))
                q[f][j] = (pz + prod[f]) + (px + rx(px, False)) + (py + ry(py, False))
                flux[f], prod[f] = fz, pz
        give(r_s, z, r)
        give(q_s, z, q)
        return (flux[0], flux[1], prod[0], prod[1])

    def finish(z, carry, k):
        r, s, hm = take(r_s, z, -1, k + 1), take(cells, z, 0, k), take(hm_s, z, 0, k)
        q, sec = take(q_s, z, 0, k), take(sec_s, z, 0, k)
        new = [{}, {}]
        for j in range(k):
            for f in range(2):
                a, c = s[f][j], r[f][j]
                near = (r[f][j + 1] + r[f][j - 1]) + (rx(c, True) + rx(c, False))
                near = near + (ry(c, True) + ry(c, False))
                inv = 2.0 * hm[f][j] - 0.5
                pulled = (3.0 * (a * a) + (6.0 * KAPPA - 1.0)) * c + COUPLE * r[1 - f][j] - KAPPA * near
                pulled = pulled + (a * inv) * (inv * q[f][j])
                new[f][j] = a + (square_w * sec[f][j] + inner_w * pulled)
        give(upd, z, new)
        return carry

    def pack(dest, c, put):
        for s in range(SLOTS):
            image = pick[SLOTS * dest + s]
            for f in range(2):
                for g in range(crow // 8):
                    start = (f * planes + HALO + c * step) * rows + g * 8 * per
                    put(s, f, pl.ds(8 * g, 8), upd[pl.ds(start + image, 8, stride=per), :])

    def exchange(c, o, to):
        return pltpu.make_async_remote_copy(
            src_ref=sbuf.at[c, o - 1], dst_ref=rbufs[c].at[pl.ds(SLOTS * to, SLOTS)],
            send_sem=as_sem.at[c, o], recv_sem=ar_sem.at[c, o],
            device_id={"img": partner(o), "slab": slab}, device_id_type=MESH,
        )

    first = HALO - 2
    dz = [moment(f, first + 1) - moment(f, first) for f in range(2)]
    carry = tuple(
        [(hm_s[at(f, first), :] + hm_s[at(f, first + 1), :]) * dz[f] for f in range(2)]
        + [(mu_s[at(f, first + 1), :] - mu_s[at(f, first), :]) * dz[f] for f in range(2)]
    )
    carry = adjoint(HALO - 1, carry, 2)

    @pl.when(jnp.logical_not(has_low))
    def _():
        for f in range(2):
            r_s[at(f, HALO - 1), :] = zero

    def chunk(c, carry):
        z = HALO + c * step
        carry = lax.fori_loop(0, step // 2, lambda i, a: adjoint(z + 1 + 2 * i, a, 2), carry)

        @pl.when(jnp.logical_not(has_high) & (c == chunks - 1))
        def _():
            for f in range(2):
                r_s[at(f, HALO + depth), :] = zero

        lax.fori_loop(0, step // 2, lambda i, a: finish(z + 2 * i, a, 2), 0)

        for k in range(chunks):
            @pl.when(c == k)
            def _():
                def ship(o):
                    def put(s, f, where, value):
                        sbuf[k, o - 1, s, f, where, :] = value

                    pack(partner(o), k, put)
                    exchange(k, o, me).start()

                each(ship)

                def keep(s, f, where, value):
                    rbufs[k][SLOTS * me + s, f, where, :] = value

                pack(me, k, keep)

        return carry

    lax.fori_loop(0, chunks, chunk, carry)

    def store(c):
        part = pl.ds(c * crow, crow)
        return pltpu.make_async_copy(outbuf.at[:, :, part, :], out.at[:, :, part, :], out_sem.at[c])

    for c in range(chunks):
        each(lambda o: exchange(c, o, partner(o)).wait_recv())

        def blend(j, carry):
            weight = (levels[j].astype(jnp.float32) + 1.0) * (1.0 / (WLEVELS + 1.0))
            one, two = where_from[2 * j], where_from[2 * j + 1]
            for f in range(2):
                outbuf[j, f, pl.ds(c * crow, crow), :] = (
                    weight * rbufs[c][one, f] + (1.0 - weight) * rbufs[c][two, f]
                )
            return carry

        lax.fori_loop(0, per, blend, 0)
        store(c).start()

    for c in range(chunks):
        each(lambda o: exchange(c, o, me).wait_send())
        store(c).wait()
    for o in range(1, m):
        share(o).wait_send()
    for c in beside:
        c.wait_send()

    @pl.when(has_high)
    def _():
        for c in to_high:
            c.wait_send()

    @pl.when(has_low)
    def _():
        for c in to_low:
            c.wait_send()


def local(n, m, state, sources, levels):
    per, _, depth, gx, gy = state.shape
    planes = depth + 2 * HALO
    chunks = depth // 4
    crow = depth // chunks * gx
    field = pltpu.VMEM((2 * planes * gx * per, gy), jnp.float32)
    flat = state.reshape(per, 2, depth * gx, gy)
    moved = pl.pallas_call(
        functools.partial(kernel, n, m, per, depth, gx, chunks),
        out_shape=jax.ShapeDtypeStruct(flat.shape, jnp.float32),
        in_specs=[pl.BlockSpec(memory_space=pltpu.HBM)] * 3,
        out_specs=pl.BlockSpec(memory_space=pl.ANY),
        scratch_shapes=[
            pltpu.SMEM((2, n * per), jnp.int32),
            pltpu.SMEM((per,), jnp.int32),
            pltpu.VMEM((per, 2, planes * gx, gy), jnp.float32),
            pltpu.VMEM((2, 2, planes * gx, gy), jnp.float32),
        ]
        + [field] * 9
        + [
            pltpu.VMEM((m, 2, per, gy), jnp.float32),
            pltpu.VMEM((per, 2, depth * gx, gy), jnp.float32),
            pltpu.SMEM((SLOTS * n,), jnp.int32),
            pltpu.SMEM((2 * per,), jnp.int32),
        ]
        + [pltpu.VMEM((chunks, n - 1, SLOTS, 2, crow, gy), jnp.float32)]
        + [pltpu.VMEM((SLOTS * n, 2, crow, gy), jnp.float32)] * chunks
        + [
            pltpu.SemaphoreType.DMA((3,)),
            pltpu.SemaphoreType.DMA((chunks,)),
            pltpu.SemaphoreType.DMA((8,)),
            pltpu.SemaphoreType.DMA((8,)),
            pltpu.SemaphoreType.DMA((m,)),
            pltpu.SemaphoreType.DMA((m,)),
            pltpu.SemaphoreType.DMA((chunks, n)),
            pltpu.SemaphoreType.DMA((chunks, n)),
        ],
        compiler_params=pltpu.CompilerParams(
            collective_id=0, has_side_effects=True, vmem_limit_bytes=48 * 1024 * 1024
        ),
        cost_estimate=pl.CostEstimate(
            flops=110 * flat.size, bytes_accessed=8 * flat.size, transcendentals=flat.size
        ),
    )(*(pltpu.with_memory_space_constraint(x, pltpu.HBM) for x in (flat, sources.T, levels)))
    return moved.reshape(state.shape)


def solution(mesh):
    return jax.shard_map(
        functools.partial(local, mesh.shape["img"], mesh.shape["slab"]),
        mesh=mesh,
        in_specs=(P("img", None, "slab", None, None), P(), P("img")),
        out_specs=P("img", None, "slab", None, None),
        check_vma=False,
    )
```

```python
import functools

import jax
import jax.numpy as jnp
from jax import lax
from jax.experimental import pallas as pl
from jax.experimental.pallas import tpu as pltpu
from jax.sharding import PartitionSpec as P

MESH = pl.DeviceIdType.MESH
WLEVELS = 16
KAPPA = 0.25
COUPLE = 0.3
STEP_SIZE = 0.004
EPSILON = 1e-06
SLOTS = 2
HALO = 4
RIM = 2


def kernel(
    n, m, per, depth, gx, chunks,
    state, sources_hbm, levels_hbm, out,
    sources, levels, land, edge, cells, mu_s, hm_s, b_s, t_s, sec_s, r_s, q_s, upd, sums, outbuf,
    pick, where_from, sbuf, *rest,
):
    rbufs = rest[:chunks]
    load_sem, out_sem, hs_sem, hr_sem, ss_sem, sr_sem, as_sem, ar_sem = rest[chunks:]
    me = lax.axis_index("img")
    slab = lax.axis_index("slab")
    entries = per * 2
    images = per * n
    planes = depth + 2 * HALO
    rows = gx * per
    step = depth // chunks
    crow = step * gx
    own = depth * gx

    def rem(a, b):
        return lax.rem(a, jnp.int32(b))

    nxt, prv = rem(me + 1, n), rem(me + n - 1, n)

    bits = [1 << k for k in range(n.bit_length() - 1)]
    turns = [bit - 2 * bit * rem(lax.div(me, jnp.int32(bit)), 2) for bit in bits]

    def partner(o):
        other = me
        for bit, turn in zip(bits, turns):
            other = other + rem(lax.div(o, jnp.int32(bit)), 2) * turn
        return other

    def each(body):
        def one(i, carry):
            body(n - 1 - i)
            return carry

        lax.fori_loop(0, n - 1, one, 0)

    has_low, has_high = slab > 0, slab < m - 1

    def loads():
        return pltpu.make_async_copy(
            state, land.at[:, :, pl.ds(HALO * gx, own), :], load_sem.at[0]
        )

    tables = [
        pltpu.make_async_copy(sources_hbm, sources, load_sem.at[1]),
        pltpu.make_async_copy(levels_hbm, levels, load_sem.at[2]),
    ]
    loads().start()
    for c in tables:
        c.start()

    barrier = pltpu.get_barrier_semaphore()

    def greet(i, s):
        pl.semaphore_signal(
            barrier, inc=1, device_id={"img": i, "slab": s}, device_id_type=MESH
        )

    each(lambda o: greet(partner(o), slab))
    for o in range(1, m):
        greet(me, rem(slab + o, m))

    @pl.when(has_low)
    def _():
        greet(nxt, slab - 1)
        greet(prv, slab - 1)

    @pl.when(has_high)
    def _():
        greet(nxt, slab + 1)
        greet(prv, slab + 1)

    count = (n - 1) + (m - 1) + jnp.where(has_low, 2, 0) + jnp.where(has_high, 2, 0)
    def settle(lo, hi):
        def body(g, carry):
            for f in range(2):
                for i in range(per):
                    cells[pl.ds((f * planes + 2 * g) * rows + i, 8, stride=per), :] = land[
                        i, f, pl.ds(pl.multiple_of(8 * g, 8), 8), :
                    ]
            return carry

        lax.fori_loop(lo // 2, hi // 2, body, 0)

    pl.semaphore_wait(barrier, count)
    for c in tables:
        c.wait()

    def halo(k, src, dst, i, s):
        return pltpu.make_async_remote_copy(
            src_ref=src, dst_ref=dst, send_sem=hs_sem.at[k], recv_sem=hr_sem.at[k],
            device_id={"img": i, "slab": s}, device_id_type=MESH,
        )

    hr, rr, top = HALO * gx, RIM * gx, (HALO + depth) * gx
    last = per - 1
    to_high = [
        halo(0, state.at[:, :, pl.ds(own - hr, hr), :], land.at[:, :, pl.ds(0, hr), :], me, slab + 1),
        halo(4, state.at[last, :, pl.ds(own - rr, rr), :], edge.at[0, :, pl.ds(hr - rr, rr), :], nxt, slab + 1),
        halo(5, state.at[0, :, pl.ds(own - rr, rr), :], edge.at[1, :, pl.ds(hr - rr, rr), :], prv, slab + 1),
    ]
    to_low = [
        halo(1, state.at[:, :, pl.ds(0, hr), :], land.at[:, :, pl.ds(top, hr), :], me, slab - 1),
        halo(6, state.at[last, :, pl.ds(0, rr), :], edge.at[0, :, pl.ds(top, rr), :], nxt, slab - 1),
        halo(7, state.at[0, :, pl.ds(0, rr), :], edge.at[1, :, pl.ds(top, rr), :], prv, slab - 1),
    ]
    beside = [
        halo(2, state.at[last], edge.at[0, :, pl.ds(hr, own), :], nxt, slab),
        halo(3, state.at[0], edge.at[1, :, pl.ds(hr, own), :], prv, slab),
    ]

    for c in beside:
        c.start()

    @pl.when(has_high)
    def _():
        for c in to_high:
            c.start()

    @pl.when(has_low)
    def _():
        for c in to_low:
            c.start()

    def rx(a, up):
        k = per if up else rows - per
        return jnp.concatenate([a[k:], a[:k]], axis=0)

    def ry(a, up):
        return pltpu.roll(a, a.shape[1] - 1 if up else 1, 1)

    def at(f, z):
        start = (f * planes + z) * rows
        return pl.ds(start if isinstance(start, int) else pl.multiple_of(start, 8), rows)

    def loop(lo, hi, body, carry, k=2):
        full = (hi - lo) // k
        if full:
            carry = lax.fori_loop(0, full, lambda i, c: body(lo + i * k, c, k), carry)
        if lo + full * k < hi:
            carry = body(lo + full * k, carry, hi - lo - full * k)
        return carry

    def take(ref, z, j0, j1):
        return [{j: ref[at(f, z + j), :] for j in range(j0, j1)} for f in range(2)]

    def give(ref, z, values):
        for f in range(2):
            for j, v in values[f].items():
                ref[at(f, z + j), :] = v

    def potentials():
        def body(z, carry, k):
            s = take(cells, z, -1, k + 1)
            mu, hm = [{}, {}], [{}, {}]
            for j in range(k):
                for f in range(2):
                    a = s[f][j]
                    sq = a * a
                    near = (s[f][j + 1] + s[f][j - 1]) + (rx(a, True) + rx(a, False))
                    near = near + (ry(a, True) + ry(a, False))
                    mu[f][j] = a * (sq + (6.0 * KAPPA - 1.0)) + COUPLE * s[1 - f][j] - KAPPA * near
                    hm[f][j] = 0.25 + 0.5 / (1.0 + sq)
            give(mu_s, z, mu)
            give(hm_s, z, hm)
            return carry

        return body

    zero = jnp.zeros((rows, 128), jnp.float32)
    loads().wait()
    settle(HALO, HALO + depth)
    potential = potentials()
    loop(HALO + 1, HALO + depth - 1, potential, 0, 3)

    def mirror(ref):
        @pl.when(jnp.logical_not(has_low))
        def _():
            for f in range(2):
                ref[at(f, HALO - 1), :] = ref[at(f, HALO), :]

        @pl.when(jnp.logical_not(has_high))
        def _():
            for f in range(2):
                ref[at(f, HALO + depth), :] = ref[at(f, HALO + depth - 1), :]

    for c in beside:
        c.wait_recv()

    line = lax.broadcasted_iota(jnp.int32, (per, 128), 0)
    at_last = line == per - 1
    at_first = line == 0

    def shifted(a, f, z):
        low, high = [], []
        for x in range(gx):
            tile = a[x * per : (x + 1) * per]
            r = pl.ds(z * gx + x, 1)
            before = jnp.broadcast_to(edge[0, f, r, :], (per, 128))
            after = jnp.broadcast_to(edge[1, f, r, :], (per, 128))
            low.append(pltpu.roll(jnp.where(at_last, before, tile), 1, 0))
            high.append(pltpu.roll(jnp.where(at_first, after, tile), per - 1, 0))
        return jnp.concatenate(low, axis=0), jnp.concatenate(high, axis=0)

    def fold(a):
        total = a[:per]
        for x in range(1, gx):
            total = total + a[x * per : (x + 1) * per]
        return total

    def z_flux(f, z):
        return (hm_s[at(f, z), :] + hm_s[at(f, z + 1), :]) * (mu_s[at(f, z + 1), :] - mu_s[at(f, z), :])

    def drifts(z, carry, k):
        flux, acc_b, acc_t = list(carry[0:2]), carry[2], carry[3]
        hm, mu, s = take(hm_s, z, 0, k + 1), take(mu_s, z, 0, k + 1), take(cells, z, 0, k)
        near = [[shifted(s[f][j], f, z + j) for j in range(k)] for f in range(2)]
        b, t, sec = [{}, {}], [{}, {}], [{}, {}]
        for j in range(k):
            for f in range(2):
                h, u = hm[f][j], mu[f][j]
                fz = (h + hm[f][j + 1]) * (mu[f][j + 1] - u)
                fx = (h + rx(h, True)) * (rx(u, True) - u)
                fy = (h + ry(h, True)) * (ry(u, True) - u)
                b[f][j] = (fz - flux[f]) + (fx - rx(fx, False)) + (fy - ry(fy, False))
                flux[f] = fz
                low, high = near[f][j]
                t[f][j] = (high - low) * ((images - 1) / 2.0)
                sec[f][j] = (high + low - 2.0 * s[f][j]) * float((images - 1) ** 2)
                inside = (z + j >= HALO) & (z + j < HALO + depth)
                counts = jnp.where(inside, jnp.float32(1.0), jnp.float32(0.0))
                acc_b = acc_b + counts * fold(b[f][j] * b[f][j])
                acc_t = acc_t + counts * fold(t[f][j] * t[f][j])
        give(b_s, z, b)
        give(t_s, z, t)
        give(sec_s, z, sec)
        return (flux[0], flux[1], acc_b, acc_t)

    none = jnp.zeros((per, 128), jnp.float32)
    def along(z, acc):
        return (z_flux(0, z - 1), z_flux(1, z - 1)) + acc

    carry = loop(HALO + 2, HALO + depth - 2, drifts, along(HALO + 2, (none, none)), 4)

    @pl.when(has_low)
    def _():
        for k in range(3):
            halo(0, *((land.at[:, :, pl.ds(0, hr), :],) * 2), me, slab - 1).wait_recv() if k == 0 else \
                halo(3 + k, *((edge.at[k - 1, :, pl.ds(hr - rr, rr), :],) * 2), me, slab - 1).wait_recv()
        settle(0, HALO)

    @pl.when(has_high)
    def _():
        for k in range(3):
            halo(1, *((land.at[:, :, pl.ds(top, hr), :],) * 2), me, slab + 1).wait_recv() if k == 0 else \
                halo(5 + k, *((edge.at[k - 1, :, pl.ds(top, rr), :],) * 2), me, slab + 1).wait_recv()
        settle(HALO + depth, planes)

    @pl.when(jnp.logical_not(has_low))
    def _():
        for f in range(2):
            for z in range(HALO):
                cells[at(f, z), :] = zero
            for k in range(2):
                edge[k, f, pl.ds(hr - rr, rr), :] = zero[:rr]

    @pl.when(jnp.logical_not(has_high))
    def _():
        for f in range(2):
            for z in range(HALO + depth, planes):
                cells[at(f, z), :] = zero
            for k in range(2):
                edge[k, f, pl.ds(top, rr), :] = zero[:rr]

    lax.fori_loop(0, 2, lambda i, c: potential(1 + i * (HALO + depth - 2), c, HALO), 0)

    mirror(mu_s)

    def outer(i, acc):
        z = HALO - 2 + i * depth
        return drifts(z, along(z, acc), 4)[2:]

    carry = (None, None) + lax.fori_loop(0, 2, outer, carry[2:])
    sums[0, 0] = carry[2]
    sums[0, 1] = carry[3]

    def share(o):
        return pltpu.make_async_remote_copy(
            src_ref=sums.at[0], dst_ref=sums.at[o], send_sem=ss_sem.at[o], recv_sem=sr_sem.at[o],
            device_id={"img": me, "slab": rem(slab + o, m)}, device_id_type=MESH,
        )

    for o in range(1, m):
        share(o).start()
    mirror(t_s)
    mirror(b_s)

    def choose(d, carry):
        seen = jnp.int32(0)
        first = jnp.int32(0)
        second = jnp.int32(0)
        for e in range(entries):
            src = sources[e % 2, d * per + e // 2]
            mine = lax.div(src, jnp.int32(per)) == me
            place = lax.rem(src, jnp.int32(per))
            first = jnp.where(mine & (seen == 0), place, first)
            second = jnp.where(mine & (seen == 1), place, second)
            seen = seen + jnp.where(mine, 1, 0)
        pick[SLOTS * d] = first
        pick[SLOTS * d + 1] = second
        return carry

    lax.fori_loop(0, n, choose, 0)
    owners = []
    for e in range(entries):
        owner = lax.div(sources[e % 2, me * per + e // 2], jnp.int32(per))
        slot = jnp.int32(0)
        for before in owners:
            slot = jnp.where(before == owner, 1, slot)
        owners.append(owner)
        where_from[e] = SLOTS * owner + slot

    for o in range(1, m):
        share(o).wait_recv()
    total_b, total_t = sums[0, 0], sums[0, 1]
    for o in range(1, m):
        total_b = total_b + sums[o, 0]
        total_t = total_t + sums[o, 1]
    total_b = jnp.sum(total_b, axis=1, keepdims=True)
    total_t = jnp.sum(total_t, axis=1, keepdims=True)
    lam = jnp.sqrt(total_b) / jnp.sqrt(total_t + EPSILON)
    lam = jnp.broadcast_to(lam, (per, 128))
    ids = line + me * per
    inner = jnp.where((ids > 0) & (ids < images - 1), STEP_SIZE, 0.0).astype(jnp.float32)

    def wide(a):
        return jnp.concatenate([a] * gx, axis=0)

    lam_w, inner_w = wide(lam), wide(inner)
    square_w = wide(inner * lam * lam)

    def moment(f, z):
        return lam_w * t_s[at(f, z), :] - b_s[at(f, z), :]

    def adjoint(z, carry, k):
        flux, prod = list(carry[0:2]), list(carry[2:4])
        hm, mu = take(hm_s, z, 0, k + 1), take(mu_s, z, 0, k + 1)
        mo = [{j: moment(f, z + j) for j in range(k + 1)} for f in range(2)]
        r, q = [{}, {}], [{}, {}]
        for j in range(k):
            for f in range(2):
                h, u, o = hm[f][j], mu[f][j], mo[f][j]
                dz, dx, dy = mo[f][j + 1] - o, rx(o, True) - o, ry(o, True) - o
                fz = (h + hm[f][j + 1]) * dz
                fx = (h + rx(h, True)) * dx
                fy = (h + ry(h, True)) * dy
                pz = (mu[f][j + 1] - u) * dz
                px = (rx(u, True) - u) * dx
                py = (ry(u, True) - u) * dy
                r[f][j] = (fz - flux[f]) + (fx - rx(fx, False)) + (fy - ry(fy, False))
                q[f][j] = (pz + prod[f]) + (px + rx(px, False)) + (py + ry(py, False))
                flux[f], prod[f] = fz, pz
        give(r_s, z, r)
        give(q_s, z, q)
        return (flux[0], flux[1], prod[0], prod[1])

    def finish(z, carry, k):
        r, s, hm = take(r_s, z, -1, k + 1), take(cells, z, 0, k), take(hm_s, z, 0, k)
        q, sec = take(q_s, z, 0, k), take(sec_s, z, 0, k)
        new = [{}, {}]
        for j in range(k):
            for f in range(2):
                a, c = s[f][j], r[f][j]
                near = (r[f][j + 1] + r[f][j - 1]) + (rx(c, True) + rx(c, False))
                near = near + (ry(c, True) + ry(c, False))
                inv = 2.0 * hm[f][j] - 0.5
                pulled = (3.0 * (a * a) + (6.0 * KAPPA - 1.0)) * c + COUPLE * r[1 - f][j] - KAPPA * near
                pulled = pulled + (a * inv) * (inv * q[f][j])
                new[f][j] = a + (square_w * sec[f][j] + inner_w * pulled)
        give(upd, z, new)
        return carry

    def pack(dest, c, put):
        for s in range(SLOTS):
            image = pick[SLOTS * dest + s]
            for f in range(2):
                for g in range(crow // 8):
                    start = (f * planes + HALO + c * step) * rows + g * 8 * per
                    put(s, f, pl.ds(8 * g, 8), upd[pl.ds(start + image, 8, stride=per), :])

    def exchange(c, o, to):
        return pltpu.make_async_remote_copy(
            src_ref=sbuf.at[c, o - 1], dst_ref=rbufs[c].at[pl.ds(SLOTS * to, SLOTS)],
            send_sem=as_sem.at[c, o], recv_sem=ar_sem.at[c, o],
            device_id={"img": partner(o), "slab": slab}, device_id_type=MESH,
        )

    first = HALO - 2
    dz = [moment(f, first + 1) - moment(f, first) for f in range(2)]
    carry = tuple(
        [(hm_s[at(f, first), :] + hm_s[at(f, first + 1), :]) * dz[f] for f in range(2)]
        + [(mu_s[at(f, first + 1), :] - mu_s[at(f, first), :]) * dz[f] for f in range(2)]
    )
    carry = adjoint(HALO - 1, carry, 2)

    @pl.when(jnp.logical_not(has_low))
    def _():
        for f in range(2):
            r_s[at(f, HALO - 1), :] = zero

    def chunk(c, carry):
        z = HALO + c * step
        carry = lax.fori_loop(0, step // 2, lambda i, a: adjoint(z + 1 + 2 * i, a, 2), carry)

        @pl.when(jnp.logical_not(has_high) & (c == chunks - 1))
        def _():
            for f in range(2):
                r_s[at(f, HALO + depth), :] = zero

        lax.fori_loop(0, step // 2, lambda i, a: finish(z + 2 * i, a, 2), 0)

        for k in range(chunks):
            @pl.when(c == k)
            def _():
                def ship(o):
                    def put(s, f, where, value):
                        sbuf[k, o - 1, s, f, where, :] = value

                    pack(partner(o), k, put)
                    exchange(k, o, me).start()

                each(ship)

                def keep(s, f, where, value):
                    rbufs[k][SLOTS * me + s, f, where, :] = value

                pack(me, k, keep)

        return carry

    lax.fori_loop(0, chunks, chunk, carry)

    def store(c):
        part = pl.ds(c * crow, crow)
        return pltpu.make_async_copy(outbuf.at[:, :, part, :], out.at[:, :, part, :], out_sem.at[c])

    for c in range(chunks):
        each(lambda o: exchange(c, o, partner(o)).wait_recv())

        def blend(j, carry):
            weight = (levels[j].astype(jnp.float32) + 1.0) * (1.0 / (WLEVELS + 1.0))
            one, two = where_from[2 * j], where_from[2 * j + 1]
            for f in range(2):
                outbuf[j, f, pl.ds(c * crow, crow), :] = (
                    weight * rbufs[c][one, f] + (1.0 - weight) * rbufs[c][two, f]
                )
            return carry

        lax.fori_loop(0, per, blend, 0)
        store(c).start()

    for c in range(chunks):
        each(lambda o: exchange(c, o, me).wait_send())
        store(c).wait()
    for o in range(1, m):
        share(o).wait_send()
    for c in beside:
        c.wait_send()

    @pl.when(has_high)
    def _():
        for c in to_high:
            c.wait_send()

    @pl.when(has_low)
    def _():
        for c in to_low:
            c.wait_send()


def local(n, m, state, sources, levels):
    per, _, depth, gx, gy = state.shape
    planes = depth + 2 * HALO
    chunks = depth // 4
    crow = depth // chunks * gx
    field = pltpu.VMEM((2 * planes * gx * per, gy), jnp.float32)
    flat = state.reshape(per, 2, depth * gx, gy)
    moved = pl.pallas_call(
        functools.partial(kernel, n, m, per, depth, gx, chunks),
        out_shape=jax.ShapeDtypeStruct(flat.shape, jnp.float32),
        in_specs=[pl.BlockSpec(memory_space=pltpu.HBM)] * 3,
        out_specs=pl.BlockSpec(memory_space=pl.ANY),
        scratch_shapes=[
            pltpu.SMEM((2, n * per), jnp.int32),
            pltpu.SMEM((per,), jnp.int32),
            pltpu.VMEM((per, 2, planes * gx, gy), jnp.float32),
            pltpu.VMEM((2, 2, planes * gx, gy), jnp.float32),
        ]
        + [field] * 9
        + [
            pltpu.VMEM((m, 2, per, gy), jnp.float32),
            pltpu.VMEM((per, 2, depth * gx, gy), jnp.float32),
            pltpu.SMEM((SLOTS * n,), jnp.int32),
            pltpu.SMEM((2 * per,), jnp.int32),
        ]
        + [pltpu.VMEM((chunks, n - 1, SLOTS, 2, crow, gy), jnp.float32)]
        + [pltpu.VMEM((SLOTS * n, 2, crow, gy), jnp.float32)] * chunks
        + [
            pltpu.SemaphoreType.DMA((3,)),
            pltpu.SemaphoreType.DMA((chunks,)),
            pltpu.SemaphoreType.DMA((8,)),
            pltpu.SemaphoreType.DMA((8,)),
            pltpu.SemaphoreType.DMA((m,)),
            pltpu.SemaphoreType.DMA((m,)),
            pltpu.SemaphoreType.DMA((chunks, n)),
            pltpu.SemaphoreType.DMA((chunks, n)),
        ],
        compiler_params=pltpu.CompilerParams(
            collective_id=0, has_side_effects=True, vmem_limit_bytes=48 * 1024 * 1024
        ),
        cost_estimate=pl.CostEstimate(
            flops=110 * flat.size, bytes_accessed=8 * flat.size, transcendentals=flat.size
        ),
    )(*(pltpu.with_memory_space_constraint(x, pltpu.HBM) for x in (flat, sources.T, levels)))
    return moved.reshape(state.shape)


def solution(mesh):
    return jax.shard_map(
        functools.partial(local, mesh.shape["img"], mesh.shape["slab"]),
        mesh=mesh,
        in_specs=(P("img", None, "slab", None, None), P(), P("img")),
        out_specs=P("img", None, "slab", None, None),
        check_vma=False,
    )
```
